128 devices in a mesh: fsdp: 8 (over x, z_lo), sp: 16 (over z_hi, y, core).
Axes of the slice: x: 4, y: 4, z: 4 (z_hi: 2, z_lo: 2; z = z_hi * 2 + z_lo), core: 2. Of those that a mesh axis runs over, the one named last changes fastest.
Arguments:
- queries: bfloat16 [8, 2, 2048, 2048], P('fsdp', None, 'sp'), may hold values from -130 to 130
- span_keys: bfloat16 [8, 2, 2048, 512], P('fsdp', None, 'sp'), may hold values from -10 to 10
- span_values: bfloat16 [8, 2, 2048, 512], P('fsdp', None, 'sp'), may hold values from -18 to 18
- cotangent: bfloat16 [8, 2, 2048, 2048], P('fsdp', None, 'sp'), may hold values from -6 to 6
- cache_keys: bfloat16 [1024, 512], P('fsdp', 'sp'), may hold values from -9 to 9
- cache_values: bfloat16 [1024, 512], P('fsdp', 'sp'), may hold values from -18 to 18
- hist_count: int32 [8], replicated, may hold values from 1 to 2
- span_ids: int32 [8, 2], replicated, may hold values from 9 to 16
Outputs:
- attended_out: bfloat16 [8, 2, 2048, 2048], P('fsdp', None, 'sp')
- grad_queries: bfloat16 [8, 2, 2048, 2048], P('fsdp', None, 'sp')
- grad_keys: bfloat16 [8, 2, 2048, 512], P('fsdp', None, 'sp')
- grad_values: bfloat16 [8, 2, 2048, 512], P('fsdp', None, 'sp')
- grad_cache_keys: float32 [1024, 512], P('fsdp', 'sp')
- grad_cache_values: float32 [1024, 512], P('fsdp', 'sp')
The draws below stay inside these ranges and needn't reach their ends.
All inputs are finite; a program needn't handle non-finite values.
Results may differ from the reference program's by a relative error of at most 0.019.
Values may be sent and summed in bfloat16 or wider, within the bound.
No kernel may reach another device: no remote copies, remote signals or barrier semaphores. Data moves between devices by JAX's collectives and lax.ppermute only.
A program may use at most 128 MiB of HBM per device.

```python
import math
import jax
import jax.numpy as jnp
from jax import lax

QH = 16
KVH = 4
HD = 128
SLOTS = 2
HB = 64
CH = 2048
HK = 1024
N_FSDP = 8


def shared_keys(key):
    return jax.random.truncated_normal(key, -6.0, 6.0, (N_FSDP, 2, CH, KVH * HD), jnp.float32)


def draw_span_keys(key, part):
    shared = shared_keys(key)
    return (1.5 * shared).astype(jnp.bfloat16)


def draw_queries(key, part):
    key = jax.random.fold_in(key, 4)
    drawn = 1.5 * jax.random.truncated_normal(jax.random.fold_in(key, 1), -6.0, 6.0, (N_FSDP, 2, CH, QH * HD), jnp.float32)
    return drawn.astype(jnp.bfloat16)


def touch_ends(values, own_key, smallest, top_value):
    index_at = [jax.random.randint(jax.random.fold_in(own_key, axis), (), 0, length) for axis, length in enumerate(values.shape)]
    main_axis = values.shape.index(max(values.shape))
    next_to = index_at[:main_axis] + [(index_at[main_axis] + 1) % values.shape[main_axis]] + index_at[main_axis + 1:]
    return values.at[tuple(index_at)].set(smallest).at[tuple(next_to)].set(top_value)


def level_of(own_key, dims, cuts, least, high):
    level = 1.0
    for dim, shards_of in cuts:
        draws = jax.random.uniform(jax.random.fold_in(jax.random.fold_in(own_key, 6), dim), (shards_of,), jnp.float32, least / len(cuts), high / len(cuts))
        level = level * jnp.repeat(jnp.exp(draws), dims[dim] // shards_of).reshape((-1,) + (1,) * (len(dims) - 1 - dim))
    return level


def bell_draw(stream_key, extent, spread, reach, pieces=(), kind=jnp.bfloat16):
    level = level_of(stream_key, extent, pieces, -0.22, 0.18) if pieces else 1.0
    array = jax.random.normal(stream_key, extent, jnp.float32) * spread * level
    return jnp.minimum(jnp.maximum(array, -reach), reach).astype(kind)


def setup_inputs(seed: int = 0) -> dict:
    streams_of = jax.random.split(jax.random.key(seed), 9)
    return {
        "queries": draw_queries(jax.random.fold_in(streams_of[8], 71), 0),
        "span_keys": draw_span_keys(jax.random.fold_in(streams_of[8], 71), 0),
        "span_values": bell_draw(streams_of[2], (N_FSDP, 2, CH, KVH * HD), 3.0, 18.0, ((0, 8), (2, 16))),
        "cotangent": bell_draw(streams_of[3], (N_FSDP, 2, CH, QH * HD), 1.0, 6.0, ((0, 8), (2, 16))),
        "cache_keys": bell_draw(streams_of[4], (HK, KVH * HD), 1.5, 9.0, ((0, 8), (1, 16))),
        "cache_values": bell_draw(streams_of[5], (HK, KVH * HD), 3.0, 18.0, ((0, 8), (1, 16))),
        "hist_count": touch_ends(jax.random.randint(streams_of[6], (N_FSDP,), 1, SLOTS + 1), jax.random.fold_in(streams_of[6], 1), 1, SLOTS).astype(jnp.int32),
        "span_ids": touch_ends(jax.random.randint(streams_of[7], (N_FSDP, 2), N_FSDP + 1, 2 * N_FSDP + 1), jax.random.fold_in(streams_of[7], 1), N_FSDP + 1, 2 * N_FSDP).astype(jnp.int32),
    }


def history_visible(hist_count, span_id):
    row_ids = jnp.arange(N_FSDP * SLOTS * HB, dtype=jnp.int32)
    owner_ids = row_ids // (SLOTS * HB)
    slot_ids = row_ids // HB % SLOTS
    row_span = slot_ids * N_FSDP + owner_ids
    owners = jnp.arange(N_FSDP, dtype=jnp.int32)
    row_count = lax.optimization_barrier(jnp.sum(jnp.where(owner_ids[:, None] == owners[None, :], hist_count[None, :], 0), axis=1))
    return (slot_ids < row_count) & (row_span < span_id)

def head_pass(query, key_rows, value_rows, grad_out, visible):
    score_scale = 1.0 / math.sqrt(query.shape[1])
    scores = jnp.dot(query, key_rows.T, preferred_element_type=jnp.float32) * score_scale
    scores = jnp.where(visible, scores, -jnp.inf)
    row_max = lax.optimization_barrier(jnp.max(scores, axis=1, keepdims=True))
    weights = jnp.exp(scores - row_max)
    row_total = lax.optimization_barrier(jnp.sum(weights, axis=1, keepdims=True))
    mixed = jnp.dot(weights.astype(jnp.bfloat16), value_rows, preferred_element_type=jnp.float32) / row_total
    attended = mixed.astype(jnp.bfloat16)
    log_total = row_max + jnp.log(row_total)
    row_delta = lax.optimization_barrier(jnp.sum(grad_out.astype(jnp.float32) * attended.astype(jnp.float32), axis=1, keepdims=True))
    probability = jnp.exp(scores - log_total)
    grad_prob = jnp.dot(grad_out, value_rows.T, preferred_element_type=jnp.float32)
    grad_score = (probability * (grad_prob - row_delta)).astype(jnp.bfloat16)
    grad_query = (jnp.dot(grad_score, key_rows, preferred_element_type=jnp.float32) * score_scale).astype(jnp.bfloat16)
    key_terms = jnp.dot(grad_score.T, query, preferred_element_type=jnp.float32) * score_scale
    value_terms = jnp.dot(probability.astype(jnp.bfloat16).T, grad_out, preferred_element_type=jnp.float32)
    return (attended, grad_query, key_terms, value_terms)

def reference(queries, span_keys, span_values, cotangent, cache_keys, cache_values, hist_count, span_ids):
    head_group = QH // KVH
    hist_keys = cache_keys.reshape(HK, KVH, HD)
    hist_values = cache_values.reshape(HK, KVH, HD)
    grad_hist_keys = jnp.zeros((KVH, HK, HD), jnp.float32)
    grad_hist_values = jnp.zeros((KVH, HK, HD), jnp.float32)
    causal = jnp.arange(CH, dtype=jnp.int32)[:, None] >= jnp.arange(CH, dtype=jnp.int32)[None, :]
    attended_list, grad_q_list, grad_k_list, grad_v_list = ([], [], [], [])
    for member in range(N_FSDP):
        attended_pair, grad_q_pair, grad_k_pair, grad_v_pair = ([], [], [], [])
        for ordinal in range(2):
            visible_hist = history_visible(hist_count, span_ids[member, ordinal])
            visible = jnp.concatenate([jnp.broadcast_to(visible_hist[None, :], (CH, HK)), causal], axis=1)
            query_heads = queries[member, ordinal].reshape(CH, QH, HD).transpose(1, 0, 2)
            grad_heads = cotangent[member, ordinal].reshape(CH, QH, HD).transpose(1, 0, 2)
            all_keys = jnp.concatenate([hist_keys, span_keys[member, ordinal].reshape(CH, KVH, HD)], axis=0).transpose(1, 0, 2)
            all_values = jnp.concatenate([hist_values, span_values[member, ordinal].reshape(CH, KVH, HD)], axis=0).transpose(1, 0, 2)

            def one_head(head_index):
                kv_head = head_index // head_group
                return head_pass(query_heads[head_index], all_keys[kv_head], all_values[kv_head], grad_heads[head_index], visible)
            attended, grad_query, key_terms, value_terms = lax.map(one_head, jnp.arange(QH, dtype=jnp.int32))
            key_sum = lax.optimization_barrier(jnp.sum(key_terms.reshape(KVH, head_group, HK + CH, HD), axis=1))
            value_sum = lax.optimization_barrier(jnp.sum(value_terms.reshape(KVH, head_group, HK + CH, HD), axis=1))
            grad_hist_keys = grad_hist_keys + key_sum[:, :HK]
            grad_hist_values = grad_hist_values + value_sum[:, :HK]
            attended_pair.append(attended.transpose(1, 0, 2).reshape(CH, QH * HD))
            grad_q_pair.append(grad_query.transpose(1, 0, 2).reshape(CH, QH * HD))
            grad_k_pair.append(key_sum[:, HK:].transpose(1, 0, 2).reshape(CH, KVH * HD).astype(jnp.bfloat16))
            grad_v_pair.append(value_sum[:, HK:].transpose(1, 0, 2).reshape(CH, KVH * HD).astype(jnp.bfloat16))
        attended_list.append(jnp.stack(attended_pair))
        grad_q_list.append(jnp.stack(grad_q_pair))
        grad_k_list.append(jnp.stack(grad_k_pair))
        grad_v_list.append(jnp.stack(grad_v_pair))
    grad_cache_keys = grad_hist_keys.transpose(1, 0, 2).reshape(HK, KVH * HD)
    grad_cache_values = grad_hist_values.transpose(1, 0, 2).reshape(HK, KVH * HD)
    return (jnp.stack(attended_list), jnp.stack(grad_q_list), jnp.stack(grad_k_list), jnp.stack(grad_v_list), grad_cache_keys, grad_cache_values)
```

```python
import functools
import math

import jax
import jax.numpy as jnp
from jax import lax
from jax.experimental import pallas as pl
from jax.experimental.pallas import tpu as pltpu
from jax.sharding import Mesh
from jax.sharding import PartitionSpec as P

BF = jnp.bfloat16
F32 = jnp.float32
HEADS = 4
KVH = 4
D = 128
TB = 128
ROWS = HEADS * TB
CK = 256
HIST = 1024
SPAN = 2048
NROW = HIST + SPAN
NCH = NROW // CK
SCALE = 1.0 / math.sqrt(D)
C2 = SCALE * math.log2(math.e)
NEG = -1e30
STEP1, STEP2, STEP3 = 4, 4, 4
SP = ("zhi", "y", "core")
FS = ("x", "zlo")


def dg(a, b, ca, cb):
    return lax.dot_general(a, b, (((ca,), (cb,)), ((), ())), preferred_element_type=F32)


def pieces(x):
    a = x.astype(BF)
    r = x - a.astype(F32)
    b = r.astype(BF)
    c = (r - b.astype(F32)).astype(BF)
    return a, b, c


def at_cols(x, rows):
    ln = lax.broadcasted_iota(jnp.int32, (rows, D), 1)
    out = jnp.zeros((rows, D), F32)
    for k, p in enumerate(pieces(x)):
        out = jnp.where(ln == k, p.astype(F32), out)
    return out


def span_kernel(
    ordinal, last, pos_ref, cnt_ref, ids_ref, qg0, qg1, qg2, qg3, kv0, kv1, kv2, kv3, hist_ref, *rest
):
    if last:
        acc_ref, *rest = rest
    (att_ref, dq_ref, dkv_ref, hg_ref, ks, vs, q_s, ga_s, qt_s, gt_s, s_s, w_s, mx, o_s, dq_s, dkt, dvt, kt, vt) = rest
    zhi, y_me, core, f_me = pos_ref[0], pos_ref[1], pos_ref[2], pos_ref[3]
    qg_refs = (qg0, qg1, qg2, qg3)
    kv_refs = (kv0, kv1, kv2, kv3)
    span_id = ids_ref[f_me, ordinal]
    see = [(cnt_ref[f] > 1) & (f + 8 < span_id) for f in range(8)]
    vs[:, D:] = jnp.ones((NROW, D), BF)
    n1 = jnp.int32(0)
    for f in range(8):
        n1 = n1 + see[f].astype(jnp.int32)
    nh1 = (n1 + 3) // 4
    ln = lax.broadcasted_iota(jnp.int32, (HIST, D), 1)
    rw = lax.broadcasted_iota(jnp.int32, (HIST, D), 0)
    ks[0:HIST, D:] = jnp.where((ln == 0) & (rw >= 512 + n1 * 64), NEG, 0.0).astype(BF)
    base = pl.multiple_of(512 + nh1 * CK, CK)
    zc = zhi * 2 + core
    n = jnp.int32(0)
    for f in range(8):
        rows = jnp.concatenate(
            [hist_ref[f, lax.rem(zc - p + 4, 4), i] for i in range(2) for p in range(4)], axis=0
        ).T
        ks[f * 64 : (f + 1) * 64, 0:D] = rows[0:64, 0:D]
        vs[f * 64 : (f + 1) * 64, 0:D] = rows[0:64, D:]
        at = pl.multiple_of(512 + n * 64, 64)
        ks[pl.ds(at, 64), 0:D] = rows[64:, 0:D]
        vs[pl.ds(at, 64), 0:D] = rows[64:, D:]
        n = n + see[f].astype(jnp.int32)
    for r in range(4):

        @pl.when(n1 + r < nh1 * 4)
        def _(r=r):
            at = pl.multiple_of(512 + (n1 + r) * 64, 64)
            ks[pl.ds(at, 64), 0:D] = jnp.zeros((64, D), BF)
            vs[pl.ds(at, 64), 0:D] = jnp.zeros((64, D), BF)

    for rel in range(4):
        z = zhi if rel < 2 else 1 - zhi
        c = core if rel % 2 == 0 else 1 - core
        for sh in range(4):
            yy = lax.rem(y_me - sh + 4, 4)
            at = pl.multiple_of(base + z * 1024 + yy * 256 + c * 128, 128)
            ks[pl.ds(at, 128), 0:D] = kv_refs[rel][sh, ordinal, :, 0:D]
            ks[pl.ds(at, 128), D:] = jnp.zeros((128, D), BF)
            vs[pl.ds(at, 128), 0:D] = kv_refs[rel][sh, ordinal, :, D:]
    kt[...] = ks[...].T
    vt[...] = vs[...].T
    dkt[...] = jnp.zeros_like(dkt)
    dvt[...] = jnp.zeros_like(dvt)
    lnr = lax.broadcasted_iota(jnp.int32, (ROWS, D), 1)
    lane = lax.broadcasted_iota(jnp.int32, (ROWS, CK), 1)
    tok = lax.broadcasted_iota(jnp.int32, (ROWS, CK), 0) % TB + core * TB
    q_s[:, D:] = jnp.where(lnr == 0, 1.0, 0.0).astype(BF)

    def chunk(i, n):
        return pl.ds(pl.multiple_of(i * CK, CK), n * CK)

    def block(sh, carry):
        b = lax.rem(y_me - sh + 4, 4)
        for s0 in range(4):

            @pl.when(sh == s0)
            def _(s0=s0):
                for h in range(HEADS):
                    q_s[h * TB : (h + 1) * TB, 0:D] = qg_refs[s0][:, h * D : (h + 1) * D]
                    ga_s[h * TB : (h + 1) * TB, 0:D] = qg_refs[s0][:, (HEADS + h) * D : (HEADS + h + 1) * D]

        mx[...] = jnp.full_like(mx, NEG)
        nfull = 2 + nh1 + zhi * 4 + b

        def walk(fn, step):
            groups = nfull // step

            def one(i, carry):
                fn(step * i, step, False)
                return carry

            lax.fori_loop(0, groups, one, 0)
            for r in range(step):

                @pl.when(nfull - groups * step == r)
                def _(r=r):
                    fn(nfull - r, r + 1, True)

        def scores(i, n, diag):
            s = dg(q_s[...], kt[:, chunk(i, n)], 1, 0)
            parts = [s[:, k * CK : (k + 1) * CK] for k in range(n)]
            if diag:
                parts[-1] = jnp.where(lane <= tok, parts[-1], NEG)
            for k in range(n):
                s_s[i + k] = parts[k]
            cols = [p[:, h * D : (h + 1) * D] for p in parts for h in range(2)]
            mx[...] = functools.reduce(jnp.maximum, cols, mx[...])

        walk(scores, STEP1)
        m = jnp.max(mx[...], axis=1, keepdims=True)
        mx[...] = jnp.broadcast_to(m * C2, (ROWS, D))
        o_s[...] = jnp.zeros_like(o_s)

        def weigh(i, n, diag):
            mm = mx[...]
            mm = jnp.concatenate([mm, mm], axis=1)
            ws = [jnp.exp2(s_s[i + k] * C2 - mm).astype(BF) for k in range(n)]
            for k in range(n):
                w_s[i + k] = ws[k]
            o_s[...] += dg(jnp.concatenate(ws, axis=1), vs[chunk(i, n), :], 1, 0)

        walk(weigh, STEP2)
        inv = 1.0 / o_s[:, D:]
        att = (o_s[:, :D] * inv).astype(BF)
        gp = (ga_s[:, 0:D].astype(F32) * inv).astype(BF)
        ga_s[:, 0:D] = gp
        for h in range(HEADS):
            att_ref[sh, :, h * D : (h + 1) * D] = att[h * TB : (h + 1) * TB, :]
        delta = jnp.sum(gp.astype(F32) * att.astype(F32), axis=1, keepdims=True)
        ga_s[:, D:] = at_cols(-delta, ROWS).astype(BF)
        qt_s[...] = q_s[:, 0:D].T
        gt_s[...] = gp.T
        dq_s[...] = jnp.zeros_like(dq_s)

        def back(i, n, diag):
            dp = dg(ga_s[...], vt[:, chunk(i, n)], 1, 0).astype(BF)
            ws = [w_s[i + k] for k in range(n)]
            dss = [ws[k] * dp[:, k * CK : (k + 1) * CK] for k in range(n)]
            dq_s[...] += dg(jnp.concatenate(dss, axis=1), ks[chunk(i, n), 0:D], 1, 0)
            for k in range(n):
                dkt[i + k] += dg(qt_s[...], dss[k], 1, 0)
                dvt[i + k] += dg(gt_s[...], ws[k], 1, 0)

        walk(back, STEP3)
        dqv = (dq_s[...] * SCALE).astype(BF)
        for h in range(HEADS):
            dq_ref[sh, :, h * D : (h + 1) * D] = dqv[h * TB : (h + 1) * TB, :]
        return carry

    lax.fori_loop(0, 4, block, 0)

    for rel in range(4):
        z = zhi if rel < 2 else 1 - zhi
        c = core if rel % 2 == 0 else 1 - core
        for sh in range(4):
            yy = lax.rem(y_me - sh + 4, 4)
            i = 2 + nh1 + z * 4 + yy
            half = pl.ds(pl.multiple_of(c * 128, 128), 128)
            dkv_ref[rel, sh, :, 0:D] = (dkt[i, :, half] * SCALE).T.astype(BF)
            dkv_ref[rel, sh, :, D:] = dvt[i, :, half].T.astype(BF)
    for i in range(4):

        @pl.when(i < 2 + nh1)
        def _(i=i):
            s_s[0, 0:CK, 0:D] = (dkt[i] * SCALE).T
            s_s[0, 0:CK, D:] = dvt[i].T
            s_s[1 + i // 2, (i % 2) * CK : (i % 2 + 1) * CK, :] = s_s[0, 0:CK, :]

    n = jnp.int32(0)
    for f in range(8):
        first = s_s[1, f * 64 : (f + 1) * 64, :]
        second = s_s[2, pl.ds(pl.multiple_of(n * 64, 64), 64), :]
        second = jnp.where(see[f], second, 0.0)
        n = n + see[f].astype(jnp.int32)
        if last:
            first = first + acc_ref[f, 0:64, :]
            second = second + acc_ref[f, 64:128, :]
            hg_ref[f] = jnp.concatenate([first, second], axis=0).T.astype(BF)
        else:
            hg_ref[f, 0:64, :] = first
            hg_ref[f, 64:128, :] = second


def span_call(ordinal, pos, cnt, ids, qgs, kvs, hist, acc=None):
    last = acc is not None
    smem = pl.BlockSpec(memory_space=pltpu.SMEM)
    vmem = pl.BlockSpec(memory_space=pltpu.VMEM)
    extra = (acc,) if last else ()
    hg = jax.ShapeDtypeStruct((8, 2 * D, TB), BF) if last else jax.ShapeDtypeStruct((8, TB, 2 * D), F32)
    return pl.pallas_call(
        functools.partial(span_kernel, ordinal, last),
        out_shape=(
            jax.ShapeDtypeStruct((4, TB, HEADS * D), BF),
            jax.ShapeDtypeStruct((4, TB, HEADS * D), BF),
            jax.ShapeDtypeStruct((4, 4, TB, 2 * D), BF),
            hg,
        ),
        in_specs=[smem] * 3 + [vmem] * (9 + len(extra)),
        out_specs=(vmem,) * 4,
        scratch_shapes=[
            pltpu.VMEM((NROW, 2 * D), BF),
            pltpu.VMEM((NROW, 2 * D), BF),
            pltpu.VMEM((ROWS, 2 * D), BF),
            pltpu.VMEM((ROWS, 2 * D), BF),
            pltpu.VMEM((D, ROWS), BF),
            pltpu.VMEM((D, ROWS), BF),
            pltpu.VMEM((NCH, ROWS, CK), F32),
            pltpu.VMEM((NCH, ROWS, CK), BF),
            pltpu.VMEM((ROWS, D), F32),
            pltpu.VMEM((ROWS, 2 * D), F32),
            pltpu.VMEM((ROWS, D), F32),
            pltpu.VMEM((NCH, D, CK), F32),
            pltpu.VMEM((NCH, D, CK), F32),
            pltpu.VMEM((2 * D, NROW), BF),
            pltpu.VMEM((2 * D, NROW), BF),
        ],
        compiler_params=pltpu.CompilerParams(vmem_limit_bytes=56 * 2**20),
        cost_estimate=pl.CostEstimate(
            flops=int(2.5e10), bytes_accessed=6 * 2**20, transcendentals=0
        ),
    )(pos, cnt, ids, *qgs, *kvs, hist, *extra)


def y_shift(a, sh):
    return lax.ppermute(a, "y", [(i, (i + sh) % 4) for i in range(4)])


def flip(a, axis):
    return lax.ppermute(a, axis, [(0, 1), (1, 0)])


def linear(z, y, c):
    return z * 8 + y * 2 + c


def per_device(queries, span_keys, span_values, cotangent, cache_keys, cache_values, hist_count, span_ids):
    zhi, y_me, core = lax.axis_index("zhi"), lax.axis_index("y"), lax.axis_index("core")
    f_me = lax.axis_index("x") * 2 + lax.axis_index("zlo")
    pos = jnp.stack([zhi, y_me, core, f_me]).astype(jnp.int32)

    def head_cols(a, sh, width):
        target = lax.rem(y_me + sh, 4)
        return lax.dynamic_slice_in_dim(a, target * width, width, axis=a.ndim - 1)

    kv_sent = [
        jnp.concatenate([head_cols(span_keys[0], sh, D), head_cols(span_values[0], sh, D)], axis=-1)
        for sh in range(4)
    ]
    kv_own = jnp.stack([kv_sent[0]] + [y_shift(kv_sent[sh], sh) for sh in (1, 2, 3)])
    cache = jnp.stack([cache_keys.T, cache_values.T])
    parts = []
    for k in range(4):
        perm = []
        for head in range(KVH):
            for piece in range(4):
                src = linear(head // 2, 2 * (head % 2) + piece // 2, piece % 2)
                to = (piece + k) % 4
                perm.append((src, linear(to // 2, head, to % 2)))
        parts.append(lax.ppermute(cache, SP, perm))
    hist = lax.all_gather(jnp.stack(parts), FS, axis=0, tiled=False).reshape(8, 4, 2, 32, TB)

    def qg_of(j):
        sent = [
            jnp.concatenate(
                [head_cols(queries[0, j], sh, HEADS * D), head_cols(cotangent[0, j], sh, HEADS * D)], axis=-1
            )
            for sh in range(4)
        ]
        return [sent[0]] + [y_shift(sent[sh], sh) for sh in (1, 2, 3)]

    qg = [qg_of(0), qg_of(1)]
    kv_core = flip(kv_own, "core")
    kv_z = flip(kv_own, "zhi")
    kv_zc = flip(kv_z, "core")
    kvs = (kv_own, kv_core, kv_z, kv_zc)
    att0, dq0, dkv0, acc = span_call(0, pos, hist_count, span_ids, qg[0], kvs, hist)
    att1, dq1, dkv1, hg = span_call(1, pos, hist_count, span_ids, qg[1], kvs, hist, acc)

    def home(a):
        got = [a[0]] + [y_shift(a[sh], 4 - sh) for sh in (1, 2, 3)]
        return place(got)

    def place(got):
        width = got[0].shape[-1]
        out = jnp.zeros(got[0].shape[:-1] + (4 * width,), got[0].dtype)
        for sh in range(4):
            out = lax.dynamic_update_slice_in_dim(out, got[sh], lax.rem(y_me + sh, 4) * width, axis=out.ndim - 1)
        return out

    def reduce_kv(dkv):
        total = dkv[0].astype(F32)
        total += flip(dkv[1], "core").astype(F32)
        total += flip(dkv[2], "zhi").astype(F32)
        both = [(linear(z, y, c), linear(1 - z, y, 1 - c)) for z in range(2) for y in range(4) for c in range(2)]
        total += lax.ppermute(dkv[3], SP, both).astype(F32)
        return total.astype(BF)

    red = jnp.stack([reduce_kv(dkv0), reduce_kv(dkv1)], axis=1)
    hg_all = lax.all_to_all(hg, FS, split_axis=0, concat_axis=0, tiled=True)
    hsum = jnp.sum(hg_all.astype(F32), axis=0).reshape(2, 4, 32, TB)
    mine = []
    for k in range(4):
        perm = []
        for head in range(KVH):
            for zc in range(4):
                piece = (zc + k) % 4
                dst = linear(head // 2, 2 * (head % 2) + piece // 2, piece % 2)
                perm.append((linear(zc // 2, head, zc % 2), dst))
        piece = lax.rem(zhi * 2 + core + k, 4)
        mine.append(lax.ppermute(lax.dynamic_index_in_dim(hsum, piece, 1, keepdims=False), SP, perm))
    hgrad = mine[0] + mine[1] + mine[2] + mine[3]
    attended = jnp.stack([home(att0), home(att1)])[None]
    grad_q = jnp.stack([home(dq0), home(dq1)])[None]
    back = [red[0]] + [y_shift(red[sh], 4 - sh) for sh in (1, 2, 3)]
    grad_k = place([b[..., 0:D] for b in back])[None]
    grad_v = place([b[..., D:] for b in back])[None]
    return attended, grad_q, grad_k, grad_v, hgrad[0].T, hgrad[1].T


def solution(mesh):
    fine = Mesh(mesh.devices.reshape(4, 2, 2, 4, 2), ("x", "zlo", "zhi", "y", "core"))
    tokens = P(FS, None, SP, None)
    resident = P(FS, SP)
    return jax.shard_map(
        per_device,
        mesh=fine,
        in_specs=(tokens,) * 4 + (resident,) * 2 + (P(), P()),
        out_specs=(tokens,) * 4 + (resident,) * 2,
        check_vma=False,
    )
```

```python
import functools
import math

import jax
import jax.numpy as jnp
from jax import lax
from jax.experimental import pallas as pl
from jax.experimental.pallas import tpu as pltpu
from jax.sharding import Mesh
from jax.sharding import PartitionSpec as P

BF = jnp.bfloat16
F32 = jnp.float32
HEADS = 4
KVH = 4
D = 128
TB = 128
ROWS = HEADS * TB
CK = 256
HIST = 1024
SPAN = 2048
NROW = HIST + SPAN
NCH = NROW // CK
SCALE = 1.0 / math.sqrt(D)
C2 = SCALE * math.log2(math.e)
NEG = -1e30
STEP1, STEP2, STEP3 = 4, 4, 4
SP = ("zhi", "y", "core")
FS = ("x", "zlo")


def dg(a, b, ca, cb):
    return lax.dot_general(a, b, (((ca,), (cb,)), ((), ())), preferred_element_type=F32)


def pieces(x):
    a = x.astype(BF)
    r = x - a.astype(F32)
    b = r.astype(BF)
    c = (r - b.astype(F32)).astype(BF)
    return a, b, c


def at_cols(x, rows):
    ln = lax.broadcasted_iota(jnp.int32, (rows, D), 1)
    out = jnp.zeros((rows, D), F32)
    for k, p in enumerate(pieces(x)):
        out = jnp.where(ln == k, p.astype(F32), out)
    return out


def span_kernel(
    ordinal, pos_ref, cnt_ref, ids_ref, qg_ref, kv0, kv1, kv2, kv3, h0, h1, *rest
):
    last = ordinal == 1
    if last:
        acc_ref, *rest = rest
    (out_ref, keep_ref, send_ref, hg_ref, *rest) = rest
    (ks, vs, q_s, ga_s, qt_s, gt_s, s_s, w_s, mx, o_s, dq_s, dkt, dvt, kt, vt) = rest
    zhi, y_me, core, x_me, zlo = pos_ref[0], pos_ref[1], pos_ref[2], pos_ref[3], pos_ref[4]
    f_me = x_me * 2 + zlo
    kv_refs = (kv0, kv1, kv2, kv3)
    span_id = ids_ref[f_me, ordinal]
    see = [(cnt_ref[f] > 1) & (f + 8 < span_id) for f in range(8)]
    vs[:, D:] = jnp.ones((NROW, D), BF)
    n1 = jnp.int32(0)
    for f in range(8):
        n1 = n1 + see[f].astype(jnp.int32)
    nh1 = (n1 + 3) // 4
    ln = lax.broadcasted_iota(jnp.int32, (HIST, D), 1)
    rw = lax.broadcasted_iota(jnp.int32, (HIST, D), 0)
    ks[0:HIST, D:] = jnp.where((ln == 0) & (rw >= 512 + n1 * 64), NEG, 0.0).astype(BF)
    base = pl.multiple_of(512 + nh1 * CK, CK)
    n = jnp.int32(0)

    def history(f, piece, i):
        c = jnp.where(core == piece % 2, 0, 1)
        at = (c, lax.rem(x_me - f // 2 + 4, 4), jnp.where(zlo == f % 2, 0, 1), i)
        return jnp.where(zhi == piece // 2, h0[at], h1[at])

    for f in range(8):
        rows = jnp.concatenate([history(f, p, i) for i in range(2) for p in range(4)], axis=0).T
        ks[f * 64 : (f + 1) * 64, 0:D] = rows[0:64, 0:D]
        vs[f * 64 : (f + 1) * 64, 0:D] = rows[0:64, D:]
        at = pl.multiple_of(512 + n * 64, 64)
        ks[pl.ds(at, 64), 0:D] = rows[64:, 0:D]
        vs[pl.ds(at, 64), 0:D] = rows[64:, D:]
        n = n + see[f].astype(jnp.int32)
    for r in range(4):

        @pl.when(n1 + r < nh1 * 4)
        def _(r=r):
            at = pl.multiple_of(512 + (n1 + r) * 64, 64)
            ks[pl.ds(at, 64), 0:D] = jnp.zeros((64, D), BF)
            vs[pl.ds(at, 64), 0:D] = jnp.zeros((64, D), BF)

    for rel in range(4):
        z = zhi if rel < 2 else 1 - zhi
        c = core if rel % 2 == 0 else 1 - core
        for sh in range(4):
            yy = lax.rem(y_me - sh + 4, 4)
            at = pl.multiple_of(base + z * 1024 + yy * 256 + c * 128, 128)
            ks[pl.ds(at, 128), 0:D] = kv_refs[rel][sh, ordinal, :, 0:D]
            ks[pl.ds(at, 128), D:] = jnp.zeros((128, D), BF)
            vs[pl.ds(at, 128), 0:D] = kv_refs[rel][sh, ordinal, :, D:]
    kt[...] = ks[...].T
    vt[...] = vs[...].T
    dkt[...] = jnp.zeros_like(dkt)
    dvt[...] = jnp.zeros_like(dvt)
    lnr = lax.broadcasted_iota(jnp.int32, (ROWS, D), 1)
    lane = lax.broadcasted_iota(jnp.int32, (ROWS, CK), 1)
    tok = lax.broadcasted_iota(jnp.int32, (ROWS, CK), 0) % TB + core * TB
    q_s[:, D:] = jnp.where(lnr == 0, 1.0, 0.0).astype(BF)

    def chunk(i, n):
        return pl.ds(pl.multiple_of(i * CK, CK), n * CK)

    def block(b, carry):
        for h in range(HEADS):
            q_s[h * TB : (h + 1) * TB, 0:D] = qg_ref[b, :, h * D : (h + 1) * D]
            ga_s[h * TB : (h + 1) * TB, 0:D] = qg_ref[b, :, (HEADS + h) * D : (HEADS + h + 1) * D]
        mx[...] = jnp.full_like(mx, NEG)
        nfull = 2 + nh1 + zhi * 4 + b

        def walk(fn, step):
            groups = nfull // step

            def one(i, carry):
                fn(step * i, step, False)
                return carry

            lax.fori_loop(0, groups, one, 0)
            for r in range(step):

                @pl.when(nfull - groups * step == r)
                def _(r=r):
                    fn(nfull - r, r + 1, True)

        def scores(i, n, diag):
            s = dg(q_s[...], kt[:, chunk(i, n)], 1, 0)
            parts = [s[:, k * CK : (k + 1) * CK] for k in range(n)]
            if diag:
                parts[-1] = jnp.where(lane <= tok, parts[-1], NEG)
            for k in range(n):
                s_s[i + k] = parts[k]
            cols = [p[:, h * D : (h + 1) * D] for p in parts for h in range(2)]
            mx[...] = functools.reduce(jnp.maximum, cols, mx[...])

        walk(scores, STEP1)
        m = jnp.max(mx[...], axis=1, keepdims=True)
        mx[...] = jnp.broadcast_to(m * C2, (ROWS, D))
        o_s[...] = jnp.zeros_like(o_s)

        def weigh(i, n, diag):
            mm = mx[...]
            mm = jnp.concatenate([mm, mm], axis=1)
            ws = [jnp.exp2(s_s[i + k] * C2 - mm).astype(BF) for k in range(n)]
            for k in range(n):
                w_s[i + k] = ws[k]
            o_s[...] += dg(jnp.concatenate(ws, axis=1), vs[chunk(i, n), :], 1, 0)

        walk(weigh, STEP2)
        inv = 1.0 / o_s[:, D:]
        att = (o_s[:, :D] * inv).astype(BF)
        gp = (ga_s[:, 0:D].astype(F32) * inv).astype(BF)
        ga_s[:, 0:D] = gp
        for h in range(HEADS):
            out_ref[b, :, h * D : (h + 1) * D] = att[h * TB : (h + 1) * TB, :]
        delta = jnp.sum(gp.astype(F32) * att.astype(F32), axis=1, keepdims=True)
        ga_s[:, D:] = at_cols(-delta, ROWS).astype(BF)
        qt_s[...] = q_s[:, 0:D].T
        gt_s[...] = gp.T
        dq_s[...] = jnp.zeros_like(dq_s)

        def back(i, n, diag):
            dp = dg(ga_s[...], vt[:, chunk(i, n)], 1, 0).astype(BF)
            ws = [w_s[i + k] for k in range(n)]
            dss = [ws[k] * dp[:, k * CK : (k + 1) * CK] for k in range(n)]
            dq_s[...] += dg(jnp.concatenate(dss, axis=1), ks[chunk(i, n), 0:D], 1, 0)
            for k in range(n):
                dkt[i + k] += dg(qt_s[...], dss[k], 1, 0)
                dvt[i + k] += dg(gt_s[...], ws[k], 1, 0)

        walk(back, STEP3)
        dqv = (dq_s[...] * SCALE).astype(BF)
        for h in range(HEADS):
            out_ref[b, :, (HEADS + h) * D : (HEADS + h + 1) * D] = dqv[h * TB : (h + 1) * TB, :]
        return carry

    lax.fori_loop(0, 4, block, 0)

    for rel in range(4):
        z = zhi if rel < 2 else 1 - zhi
        c = core if rel % 2 == 0 else 1 - core
        for sh in range(4):
            yy = lax.rem(y_me - sh + 4, 4)
            i = 2 + nh1 + z * 4 + yy
            half = pl.ds(pl.multiple_of(c * 128, 128), 128)
            if last:
                ref, at = (keep_ref, send_ref)[rel % 2], rel // 2
            else:
                ref, at = (keep_ref, send_ref)[rel // 2], rel % 2
            ref[at, sh, :, 0:D] = (dkt[i, :, half] * SCALE).T.astype(BF)
            ref[at, sh, :, D:] = dvt[i, :, half].T.astype(BF)
    for i in range(4):

        @pl.when(i < 2 + nh1)
        def _(i=i):
            s_s[0, 0:CK, 0:D] = (dkt[i] * SCALE).T
            s_s[0, 0:CK, D:] = dvt[i].T
            s_s[1 + i // 2, (i % 2) * CK : (i % 2 + 1) * CK, :] = s_s[0, 0:CK, :]

    n = jnp.int32(0)
    for f in range(8):
        first = s_s[1, f * 64 : (f + 1) * 64, :]
        second = s_s[2, pl.ds(pl.multiple_of(n * 64, 64), 64), :]
        second = jnp.where(see[f], second, 0.0)
        n = n + see[f].astype(jnp.int32)
        if last:
            first = first + acc_ref[f, 0:64, :]
            second = second + acc_ref[f, 64:128, :]
            hg_ref[f] = jnp.concatenate([first, second], axis=0).T.astype(BF)
        else:
            hg_ref[f, 0:64, :] = first
            hg_ref[f, 64:128, :] = second


def span_call(ordinal, pos, cnt, ids, qg, kvs, hist, acc=None):
    last = ordinal == 1
    smem = pl.BlockSpec(memory_space=pltpu.SMEM)
    vmem = pl.BlockSpec(memory_space=pltpu.VMEM)
    extra = (acc,) if last else ()
    hg = jax.ShapeDtypeStruct((8, 2 * D, TB), BF) if last else jax.ShapeDtypeStruct((8, TB, 2 * D), F32)
    return pl.pallas_call(
        functools.partial(span_kernel, ordinal),
        out_shape=(jax.ShapeDtypeStruct((4, TB, 2 * HEADS * D), BF),)
        + (jax.ShapeDtypeStruct((2, 4, TB, 2 * D), BF),) * 2
        + (hg,),
        in_specs=[smem] * 3 + [vmem] * (7 + len(extra)),
        out_specs=(vmem,) * 4,
        scratch_shapes=[
            pltpu.VMEM((NROW, 2 * D), BF),
            pltpu.VMEM((NROW, 2 * D), BF),
            pltpu.VMEM((ROWS, 2 * D), BF),
            pltpu.VMEM((ROWS, 2 * D), BF),
            pltpu.VMEM((D, ROWS), BF),
            pltpu.VMEM((D, ROWS), BF),
            pltpu.VMEM((NCH, ROWS, CK), F32),
            pltpu.VMEM((NCH, ROWS, CK), BF),
            pltpu.VMEM((ROWS, D), F32),
            pltpu.VMEM((ROWS, 2 * D), F32),
            pltpu.VMEM((ROWS, D), F32),
            pltpu.VMEM((NCH, D, CK), F32),
            pltpu.VMEM((NCH, D, CK), F32),
            pltpu.VMEM((2 * D, NROW), BF),
            pltpu.VMEM((2 * D, NROW), BF),
        ],
        compiler_params=pltpu.CompilerParams(vmem_limit_bytes=56 * 2**20),
        cost_estimate=pl.CostEstimate(flops=int(2.5e10), bytes_accessed=6 * 2**20, transcendentals=0),
    )(pos, cnt, ids, qg, *kvs, *hist, *extra)


def split_shifts_kernel(pos_ref, a_ref, b_ref, *outs):
    for sh in range(4):
        at = pl.ds(pl.multiple_of(lax.rem(pos_ref[1] + sh, 4) * D, D), D)
        for j in range(2):
            outs[sh][j, :, 0:D] = a_ref[0, j, :, at]
            outs[sh][j, :, D:] = b_ref[0, j, :, at]


def join_shifts_kernel(pos_ref, p0, p1, p2, p3, a_ref, b_ref):
    for sh, part in enumerate((p0, p1, p2, p3)):
        at = pl.ds(pl.multiple_of(lax.rem(pos_ref[1] + sh, 4) * D, D), D)
        for j in range(2):
            a_ref[0, j, :, at] = part[j, :, 0:D]
            b_ref[0, j, :, at] = part[j, :, D:]


def split_heads_kernel(a_ref, b_ref, out0, out1):
    width = HEADS * D
    for j, out in enumerate((out0, out1)):
        for y in range(4):
            out[y, :, 0:width] = a_ref[0, j, :, y * width : (y + 1) * width]
            out[y, :, width:] = b_ref[0, j, :, y * width : (y + 1) * width]


def join_heads_kernel(in0, in1, a_ref, b_ref):
    width = HEADS * D
    for j, part in enumerate((in0, in1)):
        for y in range(4):
            a_ref[0, j, :, y * width : (y + 1) * width] = part[y, :, 0:width]
            b_ref[0, j, :, y * width : (y + 1) * width] = part[y, :, width:]


def relayout(kernel, outs, args, with_pos):
    vmem = pl.BlockSpec(memory_space=pltpu.VMEM)
    specs = [vmem] * len(args)
    if with_pos:
        specs[0] = pl.BlockSpec(memory_space=pltpu.SMEM)
    size = 2 * sum(a.size * 2 for a in args)
    return pl.pallas_call(
        kernel,
        out_shape=tuple(jax.ShapeDtypeStruct(o, BF) for o in outs),
        in_specs=specs,
        out_specs=(vmem,) * len(outs),
        cost_estimate=pl.CostEstimate(flops=0, bytes_accessed=size, transcendentals=0),
        compiler_params=pltpu.CompilerParams(vmem_limit_bytes=16 * 2**20),
    )(*args)


def y_exchange(a):
    return lax.all_to_all(a, "y", split_axis=0, concat_axis=0, tiled=True)


def y_shift(a, sh):
    return lax.ppermute(a, "y", [(i, (i + sh) % 4) for i in range(4)])


def flip(a, axis):
    return lax.ppermute(a, axis, [(0, 1), (1, 0)])


def linear(z, y, c):
    return z * 8 + y * 2 + c


def per_device(queries, span_keys, span_values, cotangent, cache_keys, cache_values, hist_count, span_ids):
    zhi, y_me, core = lax.axis_index("zhi"), lax.axis_index("y"), lax.axis_index("core")
    pos = jnp.stack([zhi, y_me, core, lax.axis_index("x"), lax.axis_index("zlo")]).astype(jnp.int32)

    cache = jnp.stack([cache_keys.T, cache_values.T])
    perm = []
    for head in range(KVH):
        for p in range(4):
            perm.append((linear(head // 2, 2 * (head % 2) + p // 2, p % 2), linear(p // 2, head, p % 2)))
    cache = lax.ppermute(cache, SP, perm)
    cache = jnp.stack([cache, flip(cache, "zlo")])
    kv_sent = relayout(split_shifts_kernel, [(2, TB, 2 * D)] * 4, (pos, span_keys, span_values), True)
    kv_own = jnp.stack([kv_sent[0]] + [y_shift(kv_sent[sh], sh) for sh in (1, 2, 3)])
    kv_own, cache = lax.optimization_barrier((kv_own, cache))
    kv_z = flip(kv_own, "zhi")
    kv_core = flip(kv_own, "core")
    kv_zc = flip(kv_z, "core")
    kvs = (kv_own, kv_core, kv_z, kv_zc)
    cache = jnp.stack([cache] + [lax.ppermute(cache, "x", [(i, (i + s) % 4) for i in range(4)]) for s in (1, 2, 3)])
    cache = jnp.stack([cache, flip(cache, "core")])
    hist = (cache, flip(cache, "zhi"))

    sent = relayout(split_heads_kernel, [(4, TB, 2 * HEADS * D)] * 2, (queries, cotangent), False)
    qg = [y_exchange(a) for a in sent]
    out0, keep0, send0, acc = span_call(0, pos, hist_count, span_ids, qg[0], kvs, hist)
    out1, keep1, send1, hg = span_call(1, pos, hist_count, span_ids, qg[1], kvs, hist, acc)

    back0 = y_exchange(out0)
    got0 = flip(send0, "zhi")
    (out1, send1, hg, back0, got0) = lax.optimization_barrier((out1, send1, hg, back0, got0))
    hg_all = lax.all_to_all(hg, FS, split_axis=0, concat_axis=0, tiled=True)
    sum0 = (keep0.astype(F32) + got0.astype(F32)).astype(BF)
    got1 = flip(send1, "core")
    got0 = flip(sum0[1], "core")
    sum1 = (keep1.astype(F32) + got1.astype(F32)).astype(BF)
    got1 = flip(sum1[1], "zhi")
    back1 = y_exchange(out1)
    red0 = sum0[0].astype(F32) + got0.astype(F32)
    red1 = sum1[0].astype(F32) + got1.astype(F32)
    red = jnp.stack([red0, red1], axis=1).astype(BF)
    kv_back = [red[0]] + [y_shift(red[sh], 4 - sh) for sh in (1, 2, 3)]

    hsum = jnp.sum(hg_all.astype(F32), axis=0).reshape(2, 4, 32, TB)
    mine = []
    for k in range(4):
        perm = []
        for head in range(KVH):
            for zc in range(4):
                piece = (zc + k) % 4
                dst = linear(head // 2, 2 * (head % 2) + piece // 2, piece % 2)
                perm.append((linear(zc // 2, head, zc % 2), dst))
        piece = lax.rem(zhi * 2 + core + k, 4)
        mine.append(lax.ppermute(lax.dynamic_index_in_dim(hsum, piece, 1, keepdims=False), SP, perm))
    hgrad = mine[0] + mine[1] + mine[2] + mine[3]
    attended, grad_q = relayout(join_heads_kernel, [(1, 2, TB, 4 * HEADS * D)] * 2, (back0, back1), False)
    grad_k, grad_v = relayout(join_shifts_kernel, [(1, 2, TB, 4 * D)] * 2, (pos, *kv_back), True)
    return attended, grad_q, grad_k, grad_v, hgrad[0].T, hgrad[1].T


def solution(mesh):
    fine = Mesh(mesh.devices.reshape(4, 2, 2, 4, 2), ("x", "zlo", "zhi", "y", "core"))
    tokens = P(FS, None, SP, None)
    resident = P(FS, SP)
    return jax.shard_map(
        per_device,
        mesh=fine,
        in_specs=(tokens,) * 4 + (resident,) * 2 + (P(), P()),
        out_specs=(tokens,) * 4 + (resident,) * 2,
        check_vma=False,
    )
```

```python
import functools
import math

import jax
import jax.numpy as jnp
from jax import lax
from jax.experimental import pallas as pl
from jax.experimental.pallas import tpu as pltpu
from jax.sharding import Mesh
from jax.sharding import PartitionSpec as P

BF = jnp.bfloat16
F32 = jnp.float32
HEADS = 4
KVH = 4
D = 128
TB = 128
ROWS = HEADS * TB
CK = 256
HIST = 1024
SPAN = 2048
NROW = HIST + SPAN
NCH = NROW // CK
SCALE = 1.0 / math.sqrt(D)
C2 = SCALE * math.log2(math.e)
NEG = -1e30
STEP1, STEP2, STEP3 = 6, 6, 6
SP = ("zhi", "y", "core")
FS = ("x", "zlo")


def dg(a, b, ca, cb):
    return lax.dot_general(a, b, (((ca,), (cb,)), ((), ())), preferred_element_type=F32)


def pieces(x):
    a = x.astype(BF)
    r = x - a.astype(F32)
    b = r.astype(BF)
    c = (r - b.astype(F32)).astype(BF)
    return a, b, c


def at_cols(x, rows):
    ln = lax.broadcasted_iota(jnp.int32, (rows, D), 1)
    out = jnp.zeros((rows, D), F32)
    for k, p in enumerate(pieces(x)):
        out = jnp.where(ln == k, p.astype(F32), out)
    return out


def span_kernel(
    ordinal, pos_ref, cnt_ref, ids_ref, *rest
):
    last = ordinal == 1
    qg_hbm, rest = (rest[:4], rest[4:]) if last else (rest[:1], rest[1:])
    gathered, rest = rest[:4], rest[4:]
    if last:
        acc_ref, *rest = rest
    first_kv = ordinal * (4 * TB + 8 * 32)
    *out_refs, keep_ref, send_ref, hg_ref = rest[:7]
    rest = rest[7:]
    (ks, vs, q_s, ga_s, qt_s, gt_s, s_s, w_s, mx, o_s, dq_s, dkt, dvt, qg_ref, o_b, h_s, sem) = rest
    zhi, y_me, core, x_me, zlo = pos_ref[0], pos_ref[1], pos_ref[2], pos_ref[3], pos_ref[4]
    f_me = x_me * 2 + zlo
    if last:
        fetches = [
            pltpu.make_async_copy(qg_hbm[sh], qg_ref.at[lax.rem(y_me - sh + 4, 4)], sem.at[sh]) for sh in range(4)
        ]
    else:
        fetches = [pltpu.make_async_copy(qg_hbm[0], qg_ref, sem.at[0])]
    for fetch in fetches:
        fetch.start()
    span_id = ids_ref[f_me, ordinal]
    see = [(cnt_ref[f] > 1) & (f + 8 < span_id) for f in range(8)]
    vs[:, D:] = jnp.ones((NROW, D), BF)
    n1 = jnp.int32(0)
    for f in range(8):
        n1 = n1 + see[f].astype(jnp.int32)
    nh1 = (n1 + 3) // 4
    ln = lax.broadcasted_iota(jnp.int32, (HIST, D), 1)
    rw = lax.broadcasted_iota(jnp.int32, (HIST, D), 0)
    ks[0:HIST, D:] = jnp.where((ln == 0) & (rw >= 512 + n1 * 64), NEG, 0.0).astype(BF)
    base = pl.multiple_of(512 + nh1 * CK, CK)
    n = jnp.int32(0)

    for rel in range(4):
        for i in range(8):
            h_s[rel, i] = gathered[rel][4 * TB + i * 32 : 4 * TB + (i + 1) * 32, :]

    def history(f, piece):
        rel = (zhi ^ (piece // 2)) * 2 + (core ^ (piece % 2))
        return h_s[rel, (zlo ^ (f % 2)) * 4 + lax.rem(x_me - f // 2 + 4, 4)]

    for f in range(8):
        cols = jnp.concatenate([history(f, p) for p in range(4)], axis=0)
        rows = jnp.concatenate([cols[:, 0:TB].T, cols[:, TB:].T], axis=1)
        ks[f * 64 : (f + 1) * 64, 0:D] = rows[0:64, 0:D]
        vs[f * 64 : (f + 1) * 64, 0:D] = rows[0:64, D:]
        at = pl.multiple_of(512 + n * 64, 64)
        ks[pl.ds(at, 64), 0:D] = rows[64:, 0:D]
        vs[pl.ds(at, 64), 0:D] = rows[64:, D:]
        n = n + see[f].astype(jnp.int32)
    for r in range(4):

        @pl.when(n1 + r < nh1 * 4)
        def _(r=r):
            at = pl.multiple_of(512 + (n1 + r) * 64, 64)
            ks[pl.ds(at, 64), 0:D] = jnp.zeros((64, D), BF)
            vs[pl.ds(at, 64), 0:D] = jnp.zeros((64, D), BF)

    for rel in range(4):
        z = zhi if rel < 2 else 1 - zhi
        c = core if rel % 2 == 0 else 1 - core
        for sh in range(4):
            yy = lax.rem(y_me - sh + 4, 4)
            at = pl.multiple_of(base + z * 1024 + yy * 256 + c * 128, 128)
            part = gathered[rel][first_kv + sh * TB : first_kv + (sh + 1) * TB, :]
            ks[pl.ds(at, 128), 0:D] = part[:, 0:D]
            ks[pl.ds(at, 128), D:] = jnp.zeros((128, D), BF)
            vs[pl.ds(at, 128), 0:D] = part[:, D:]
    dkt[...] = jnp.zeros_like(dkt)
    dvt[...] = jnp.zeros_like(dvt)
    lnr = lax.broadcasted_iota(jnp.int32, (ROWS, D), 1)
    lane = lax.broadcasted_iota(jnp.int32, (ROWS, CK), 1)
    tok = lax.broadcasted_iota(jnp.int32, (ROWS, CK), 0) % TB + core * TB
    q_s[:, D:] = jnp.where(lnr == 0, 1.0, 0.0).astype(BF)

    def chunk(i, n):
        return pl.ds(pl.multiple_of(i * CK, CK), n * CK)

    def block(b, carry):
        for h in range(HEADS):
            q_s[h * TB : (h + 1) * TB, 0:D] = qg_ref[b, :, h * D : (h + 1) * D]
            ga_s[h * TB : (h + 1) * TB, 0:D] = qg_ref[b, :, (HEADS + h) * D : (HEADS + h + 1) * D]
        mx[...] = jnp.full_like(mx, NEG)
        nfull = 2 + nh1 + zhi * 4 + b

        def walk(fn, step):
            groups = nfull // step

            def one(i, carry):
                fn(step * i, step, False)
                return carry

            lax.fori_loop(0, groups, one, 0)
            for r in range(step):

                @pl.when(nfull - groups * step == r)
                def _(r=r):
                    fn(nfull - r, r + 1, True)

        def scores(i, n, diag):
            s = dg(q_s[...], ks[chunk(i, n), :], 1, 1)
            parts = [s[:, k * CK : (k + 1) * CK] for k in range(n)]
            if diag:
                parts[-1] = jnp.where(lane <= tok, parts[-1], NEG)
            for k in range(n):
                s_s[i + k] = parts[k]
            cols = [p[:, h * D : (h + 1) * D] for p in parts for h in range(2)]
            mx[...] = functools.reduce(jnp.maximum, cols, mx[...])

        walk(scores, STEP1)
        m = jnp.max(mx[...], axis=1, keepdims=True)
        mx[...] = jnp.broadcast_to(m * C2, (ROWS, D))
        o_s[...] = jnp.zeros_like(o_s)

        def weigh(i, n, diag):
            mm = mx[...]
            mm = jnp.concatenate([mm, mm], axis=1)
            ws = [jnp.exp2(s_s[i + k] * C2 - mm).astype(BF) for k in range(n)]
            for k in range(n):
                w_s[i + k] = ws[k]
            o_s[...] += dg(jnp.concatenate(ws, axis=1), vs[chunk(i, n), :], 1, 0)

        walk(weigh, STEP2)
        inv = 1.0 / o_s[:, D:]
        att = (o_s[:, :D] * inv).astype(BF)
        gp = (ga_s[:, 0:D].astype(F32) * inv).astype(BF)
        ga_s[:, 0:D] = gp
        for h in range(HEADS):
            o_b[:, h * D : (h + 1) * D] = att[h * TB : (h + 1) * TB, :]
        delta = jnp.sum(gp.astype(F32) * att.astype(F32), axis=1, keepdims=True)
        ga_s[:, D:] = at_cols(-delta, ROWS).astype(BF)
        qt_s[...] = q_s[:, 0:D].T
        gt_s[...] = gp.T
        dq_s[...] = jnp.zeros_like(dq_s)

        def back(i, n, diag):
            dp = dg(ga_s[...], vs[chunk(i, n), :], 1, 1).astype(BF)
            ws = [w_s[i + k] for k in range(n)]
            dss = [ws[k] * dp[:, k * CK : (k + 1) * CK] for k in range(n)]
            dq_s[...] += dg(jnp.concatenate(dss, axis=1), ks[chunk(i, n), 0:D], 1, 0)
            for k in range(n):
                dkt[i + k] += dg(qt_s[...], dss[k], 1, 0)
                dvt[i + k] += dg(gt_s[...], ws[k], 1, 0)

        walk(back, STEP3)
        dqv = (dq_s[...] * SCALE).astype(BF)
        for h in range(HEADS):
            o_b[:, (HEADS + h) * D : (HEADS + h + 1) * D] = dqv[h * TB : (h + 1) * TB, :]
        for sh in range(4):

            @pl.when(lax.rem(y_me - b + 4, 4) == sh)
            def _(sh=sh):
                out_refs[sh][...] = o_b[...]

        return carry

    for fetch in fetches:
        fetch.wait()
    lax.fori_loop(0, 4, block, 0)

    for rel in range(4):
        z = zhi if rel < 2 else 1 - zhi
        c = core if rel % 2 == 0 else 1 - core
        for sh in range(4):
            yy = lax.rem(y_me - sh + 4, 4)
            i = 2 + nh1 + z * 4 + yy
            half = pl.ds(pl.multiple_of(c * 128, 128), 128)
            if last:
                ref, at = (keep_ref, send_ref)[rel % 2], rel // 2
            else:
                ref, at = (keep_ref, send_ref)[rel // 2], rel % 2
            ref[at, sh, :, 0:D] = (dkt[i, :, half] * SCALE).T.astype(BF)
            ref[at, sh, :, D:] = dvt[i, :, half].T.astype(BF)
    for i in range(4):

        @pl.when(i < 2 + nh1)
        def _(i=i):
            s_s[0, 0:CK, 0:D] = (dkt[i] * SCALE).T
            s_s[0, 0:CK, D:] = dvt[i].T
            s_s[1 + i // 2, (i % 2) * CK : (i % 2 + 1) * CK, :] = s_s[0, 0:CK, :]

    n = jnp.int32(0)
    for f in range(8):
        first = s_s[1, f * 64 : (f + 1) * 64, :]
        second = s_s[2, pl.ds(pl.multiple_of(n * 64, 64), 64), :]
        second = jnp.where(see[f], second, 0.0)
        n = n + see[f].astype(jnp.int32)
        if last:
            first = first + acc_ref[f, 0:64, :]
            second = second + acc_ref[f, 64:128, :]
            both = jnp.concatenate([first, second], axis=0).T.astype(BF)
            for p in range(4):
                hg_ref[f, p, 0] = both[p * 32 : (p + 1) * 32]
                hg_ref[f, p, 1] = both[D + p * 32 : D + (p + 1) * 32]
        else:
            hg_ref[f, 0:64, :] = first
            hg_ref[f, 64:128, :] = second


def span_call(ordinal, pos, cnt, ids, qg, gathered, acc=None):
    last = ordinal == 1
    smem = pl.BlockSpec(memory_space=pltpu.SMEM)
    vmem = pl.BlockSpec(memory_space=pltpu.VMEM)
    extra = (acc,) if last else ()
    out = (jax.ShapeDtypeStruct((TB, 2 * HEADS * D), BF),) * 4
    hg = jax.ShapeDtypeStruct((8, 4, 2, 32, TB), BF) if last else jax.ShapeDtypeStruct((8, TB, 2 * D), F32)
    return pl.pallas_call(
        functools.partial(span_kernel, ordinal),
        out_shape=out
        + (jax.ShapeDtypeStruct((2, 4, TB, 2 * D), BF),) * 2
        + (hg,),
        in_specs=[smem] * 3 + [pl.BlockSpec(memory_space=pl.ANY)] * len(qg) + [vmem] * (4 + len(extra)),
        out_specs=(vmem,) * (len(out) + 3),
        scratch_shapes=[
            pltpu.VMEM((NROW, 2 * D), BF),
            pltpu.VMEM((NROW, 2 * D), BF),
            pltpu.VMEM((ROWS, 2 * D), BF),
            pltpu.VMEM((ROWS, 2 * D), BF),
            pltpu.VMEM((D, ROWS), BF),
            pltpu.VMEM((D, ROWS), BF),
            pltpu.VMEM((NCH, ROWS, CK), F32),
            pltpu.VMEM((NCH, ROWS, CK), BF),
            pltpu.VMEM((ROWS, D), F32),
            pltpu.VMEM((ROWS, 2 * D), F32),
            pltpu.VMEM((ROWS, D), F32),
            pltpu.VMEM((NCH, D, CK), F32),
            pltpu.VMEM((NCH, D, CK), F32),
            pltpu.VMEM((4, TB, 2 * HEADS * D), BF),
            pltpu.VMEM((TB, 2 * HEADS * D), BF),
            pltpu.VMEM((4, 8, 32, 2 * D), BF),
            pltpu.SemaphoreType.DMA((4,)),
        ],
        compiler_params=pltpu.CompilerParams(vmem_limit_bytes=40 * 2**20),
        cost_estimate=pl.CostEstimate(flops=int(2.5e10), bytes_accessed=6 * 2**20, transcendentals=0),
    )(pos, cnt, ids, *qg, *gathered, *extra)


def split_shifts_kernel(pos_ref, a_ref, b_ref, *outs):
    for sh in range(4):
        at = pl.ds(pl.multiple_of(lax.rem(pos_ref[1] + sh, 4) * D, D), D)
        for j in range(2):
            outs[sh][j, :, 0:D] = a_ref[0, j, :, at]
            outs[sh][j, :, D:] = b_ref[0, j, :, at]


def join_shifts_kernel(pos_ref, p0, p1, p2, p3, a_ref, b_ref):
    for sh, part in enumerate((p0, p1, p2, p3)):
        at = pl.ds(pl.multiple_of(lax.rem(pos_ref[1] + sh, 4) * D, D), D)
        for j in range(2):
            a_ref[0, j, :, at] = part[j, :, 0:D]
            b_ref[0, j, :, at] = part[j, :, D:]


def copy_all(pairs, sem):
    copies = [pltpu.make_async_copy(src, dst, sem.at[i]) for i, (src, dst) in enumerate(pairs)]
    for c in copies:
        c.start()
    for c in copies:
        c.wait()


def split_heads_kernel(pos_ref, a_ref, b_ref, out0, s0, s1, s2, s3, sem):
    width = HEADS * D
    pairs = []
    for y in range(4):
        at = pl.ds(y * width, width)
        pairs.append((a_ref.at[0, 0, :, at], out0.at[y, :, pl.ds(0, width)]))
        pairs.append((b_ref.at[0, 0, :, at], out0.at[y, :, pl.ds(width, width)]))
    for sh, part in enumerate((s0, s1, s2, s3)):
        at = pl.ds(pl.multiple_of(lax.rem(pos_ref[1] + sh, 4) * width, D), width)
        pairs.append((a_ref.at[0, 1, :, at], part.at[:, pl.ds(0, width)]))
        pairs.append((b_ref.at[0, 1, :, at], part.at[:, pl.ds(width, width)]))
    copy_all(pairs, sem)


def join_heads_kernel(pos_ref, *refs):
    width = HEADS * D
    a_ref, b_ref, sem = refs[8:]
    pairs = []
    for sh in range(4):
        at = pl.ds(pl.multiple_of(lax.rem(pos_ref[1] + sh, 4) * width, D), width)
        for j in range(2):
            pairs.append((refs[4 * j + sh].at[:, pl.ds(0, width)], a_ref.at[0, j, :, at]))
            pairs.append((refs[4 * j + sh].at[:, pl.ds(width, width)], b_ref.at[0, j, :, at]))
    copy_all(pairs, sem)


def relayout(kernel, outs, args, with_pos, copies=0):
    ref = pl.BlockSpec(memory_space=pl.ANY if copies else pltpu.VMEM)
    specs = [ref] * len(args)
    if with_pos:
        specs[0] = pl.BlockSpec(memory_space=pltpu.SMEM)
    size = 2 * sum(a.size * 2 for a in args)
    return pl.pallas_call(
        kernel,
        out_shape=tuple(jax.ShapeDtypeStruct(o, BF) for o in outs),
        in_specs=specs,
        out_specs=(ref,) * len(outs),
        scratch_shapes=[pltpu.SemaphoreType.DMA((copies,))] if copies else [],
        cost_estimate=pl.CostEstimate(flops=0, bytes_accessed=size, transcendentals=0),
        compiler_params=pltpu.CompilerParams(vmem_limit_bytes=16 * 2**20),
    )(*args)


def y_exchange(a):
    return lax.all_to_all(a, "y", split_axis=0, concat_axis=0, tiled=True)


def y_shift(a, sh):
    return lax.ppermute(a, "y", [(i, (i + sh) % 4) for i in range(4)])


def flip(a, axis):
    return lax.ppermute(a, axis, [(0, 1), (1, 0)])


def linear(z, y, c):
    return z * 8 + y * 2 + c


def per_device(queries, span_keys, span_values, cotangent, cache_keys, cache_values, hist_count, span_ids):
    zhi, y_me, core = lax.axis_index("zhi"), lax.axis_index("y"), lax.axis_index("core")
    pos = jnp.stack([zhi, y_me, core, lax.axis_index("x"), lax.axis_index("zlo")]).astype(jnp.int32)

    cache = jnp.concatenate([cache_keys.T, cache_values.T], axis=1)
    perm = []
    for head in range(KVH):
        for p in range(4):
            perm.append((linear(head // 2, 2 * (head % 2) + p // 2, p % 2), linear(p // 2, head, p % 2)))
    cache = lax.ppermute(cache, SP, perm)
    cache = jnp.stack([cache] + [lax.ppermute(cache, "x", [(i, (i + s) % 4) for i in range(4)]) for s in (1, 2, 3)])
    cache_x = cache
    cache = jnp.stack([cache, flip(cache, "zlo")]).reshape(8 * 32, 2 * D)
    kv_sent = relayout(split_shifts_kernel, [(2, TB, 2 * D)] * 4, (pos, span_keys, span_values), True)
    queries, kv_sent = lax.optimization_barrier((queries, kv_sent))
    wide = (TB, 2 * HEADS * D)
    sent0, *sent1 = relayout(
        split_heads_kernel, [(4,) + wide] + [wide] * 4, (pos, queries, cotangent), True, 16
    )
    kv_here = [kv_sent[0]] + [y_shift(kv_sent[sh], sh) for sh in (1, 2, 3)]
    own = jnp.concatenate([a[0] for a in kv_here] + [cache] + [a[1] for a in kv_here], axis=0)
    sent0, own = lax.optimization_barrier((sent0, own))
    qg0 = y_exchange(sent0)
    other = flip(own, "zhi")
    gathered = (own, flip(own, "core"), other, flip(other, "core"))
    sent1, _ = lax.optimization_barrier((sent1, other))
    qg1 = [sent1[0]] + [y_shift(sent1[sh], sh) for sh in (1, 2, 3)]
    out0 = span_call(0, pos, hist_count, span_ids, (qg0,), gathered)
    *out0, keep0, send0, acc = out0
    *out1, keep1, send1, hg = span_call(1, pos, hist_count, span_ids, qg1, gathered, acc)

    back0 = [out0[0]] + [y_shift(out0[sh], 4 - sh) for sh in (1, 2, 3)]
    got0 = flip(send0, "zhi")
    (out1, send1, hg, back0, got0) = lax.optimization_barrier((out1, send1, hg, back0, got0))
    sum0 = (keep0.astype(F32) + got0.astype(F32)).astype(BF)
    got1 = flip(send1, "core")
    back1 = [out1[0]] + [y_shift(out1[sh], 4 - sh) for sh in (1, 2, 3)]
    sum1 = (keep1.astype(F32) + got1.astype(F32)).astype(BF)
    hg, sum1 = lax.optimization_barrier((hg, sum1))
    hg = lax.all_to_all(hg.reshape(32, 2, 32, TB), FS + ("zhi", "core"), split_axis=0, concat_axis=0, tiled=True)
    got0 = flip(sum0[1], "core")
    got1 = flip(sum1[1], "zhi")
    red0 = sum0[0].astype(F32) + got0.astype(F32)
    red1 = sum1[0].astype(F32) + got1.astype(F32)
    red = jnp.stack([red0, red1], axis=1).astype(BF)
    back1, red = lax.optimization_barrier((back1, red))
    kv_back = [red[0]] + [y_shift(red[sh], 4 - sh) for sh in (1, 2, 3)]

    hgrad = lax.ppermute(jnp.sum(hg.astype(F32), axis=0), SP, [(b, a) for a, b in perm])
    attended, grad_q = relayout(join_heads_kernel, [(1, 2, TB, 4 * HEADS * D)] * 2, (pos, *back0, *back1), True, 16)
    grad_k, grad_v = relayout(join_shifts_kernel, [(1, 2, TB, 4 * D)] * 2, (pos, *kv_back), True)
    return attended, grad_q, grad_k, grad_v, hgrad[0].T, hgrad[1].T


def solution(mesh):
    fine = Mesh(mesh.devices.reshape(4, 2, 2, 4, 2), ("x", "zlo", "zhi", "y", "core"))
    tokens = P(FS, None, SP, None)
    resident = P(FS, SP)
    return jax.shard_map(
        per_device,
        mesh=fine,
        in_specs=(tokens,) * 4 + (resident,) * 2 + (P(), P()),
        out_specs=(tokens,) * 4 + (resident,) * 2,
        check_vma=False,
    )
```

```python
import functools
import math

import jax
import jax.numpy as jnp
from jax import lax
from jax.experimental import pallas as pl
from jax.experimental.pallas import tpu as pltpu
from jax.sharding import Mesh
from jax.sharding import PartitionSpec as P

BF = jnp.bfloat16
F32 = jnp.float32
HEADS = 4
KVH = 4
D = 128
TB = 128
ROWS = HEADS * TB
CK = 256
HIST = 1024
SPAN = 2048
NROW = HIST + SPAN
NCH = NROW // CK
SCALE = 1.0 / math.sqrt(D)
C2 = SCALE * math.log2(math.e)
NEG = -1e30
STEP1, STEP2, STEP3 = 5, 5, 5
SP = ("zhi", "y", "core")
FS = ("x", "zlo")


def dg(a, b, ca, cb):
    return lax.dot_general(a, b, (((ca,), (cb,)), ((), ())), preferred_element_type=F32)


def pieces(x):
    a = x.astype(BF)
    r = x - a.astype(F32)
    b = r.astype(BF)
    c = (r - b.astype(F32)).astype(BF)
    return a, b, c


def at_cols(x, rows):
    ln = lax.broadcasted_iota(jnp.int32, (rows, D), 1)
    out = jnp.zeros((rows, D), F32)
    for k, p in enumerate(pieces(x)):
        out = jnp.where(ln == k, p.astype(F32), out)
    return out


def span_kernel(
    ordinal, pos_ref, cnt_ref, ids_ref, *rest
):
    last = ordinal == 1
    qg_hbm, rest = (rest[:4], rest[4:]) if last else (rest[:1], rest[1:])
    gathered, rest = rest[:4], rest[4:]
    if last:
        acc_ref, *rest = rest
    first_kv = ordinal * (4 * TB + 8 * 32)
    *out_refs, keep_ref, send_ref, hg_ref = rest[:7]
    rest = rest[7:]
    (ks, vs, q_s, ga_s, qt_s, gt_s, s_s, w_s, mx, o_s, dq_s, dkt, dvt, qg_ref, o_b, h_s, sem) = rest
    zhi, y_me, core, x_me, zlo = pos_ref[0], pos_ref[1], pos_ref[2], pos_ref[3], pos_ref[4]
    f_me = x_me * 2 + zlo
    if last:
        fetches = [
            pltpu.make_async_copy(qg_hbm[sh], qg_ref.at[lax.rem(y_me - sh + 4, 4)], sem.at[sh]) for sh in range(4)
        ]
    else:
        fetches = [pltpu.make_async_copy(qg_hbm[0], qg_ref, sem.at[0])]
    for fetch in fetches:
        fetch.start()
    span_id = ids_ref[f_me, ordinal]
    see = [(cnt_ref[f] > 1) & (f + 8 < span_id) for f in range(8)]
    vs[:, D:] = jnp.ones((NROW, D), BF)
    n1 = jnp.int32(0)
    for f in range(8):
        n1 = n1 + see[f].astype(jnp.int32)
    nh1 = (n1 + 3) // 4
    ln = lax.broadcasted_iota(jnp.int32, (HIST, D), 1)
    rw = lax.broadcasted_iota(jnp.int32, (HIST, D), 0)
    ks[0:HIST, D:] = jnp.where((ln == 0) & (rw >= 512 + n1 * 64), NEG, 0.0).astype(BF)
    base = pl.multiple_of(512 + nh1 * CK, CK)
    n = jnp.int32(0)

    for rel in range(4):
        for i in range(8):
            h_s[rel, i] = gathered[rel][4 * TB + i * 32 : 4 * TB + (i + 1) * 32, :]

    def history(f, piece):
        rel = (zhi ^ (piece // 2)) * 2 + (core ^ (piece % 2))
        return h_s[rel, (zlo ^ (f % 2)) * 4 + lax.rem(x_me - f // 2 + 4, 4)]

    for f in range(8):
        cols = jnp.concatenate([history(f, p) for p in range(4)], axis=0)
        rows = jnp.concatenate([cols[:, 0:TB].T, cols[:, TB:].T], axis=1)
        ks[f * 64 : (f + 1) * 64, 0:D] = rows[0:64, 0:D]
        vs[f * 64 : (f + 1) * 64, 0:D] = rows[0:64, D:]
        at = pl.multiple_of(512 + n * 64, 64)
        ks[pl.ds(at, 64), 0:D] = rows[64:, 0:D]
        vs[pl.ds(at, 64), 0:D] = rows[64:, D:]
        n = n + see[f].astype(jnp.int32)
    for r in range(4):

        @pl.when(n1 + r < nh1 * 4)
        def _(r=r):
            at = pl.multiple_of(512 + (n1 + r) * 64, 64)
            ks[pl.ds(at, 64), 0:D] = jnp.zeros((64, D), BF)
            vs[pl.ds(at, 64), 0:D] = jnp.zeros((64, D), BF)

    for rel in range(4):
        z = zhi if rel < 2 else 1 - zhi
        c = core if rel % 2 == 0 else 1 - core
        for sh in range(4):
            yy = lax.rem(y_me - sh + 4, 4)
            at = pl.multiple_of(base + z * 1024 + yy * 256 + c * 128, 128)
            part = gathered[rel][first_kv + sh * TB : first_kv + (sh + 1) * TB, :]
            ks[pl.ds(at, 128), 0:D] = part[:, 0:D]
            ks[pl.ds(at, 128), D:] = jnp.zeros((128, D), BF)
            vs[pl.ds(at, 128), 0:D] = part[:, D:]
    dkt[...] = jnp.zeros_like(dkt)
    dvt[...] = jnp.zeros_like(dvt)
    lnr = lax.broadcasted_iota(jnp.int32, (ROWS, D), 1)
    lane = lax.broadcasted_iota(jnp.int32, (ROWS, CK), 1)
    tok = lax.broadcasted_iota(jnp.int32, (ROWS, CK), 0) % TB + core * TB
    q_s[:, D:] = jnp.where(lnr == 0, 1.0, 0.0).astype(BF)

    def chunk(i, n):
        return pl.ds(pl.multiple_of(i * CK, CK), n * CK)

    def block(b, carry):
        for h in range(HEADS):
            q_s[h * TB : (h + 1) * TB, 0:D] = qg_ref[b, :, h * D : (h + 1) * D]
            ga_s[h * TB : (h + 1) * TB, 0:D] = qg_ref[b, :, (HEADS + h) * D : (HEADS + h + 1) * D]
        mx[...] = jnp.full_like(mx, NEG)
        nfull = 2 + nh1 + zhi * 4 + b

        def walk(fn, step):
            groups = nfull // step

            def one(i, carry):
                fn(step * i, step, False)
                return carry

            lax.fori_loop(0, groups, one, 0)
            for r in range(step):

                @pl.when(nfull - groups * step == r)
                def _(r=r):
                    fn(nfull - r, r + 1, True)

        def scores(i, n, diag):
            s = dg(q_s[...], ks[chunk(i, n), :], 1, 1)
            parts = [s[:, k * CK : (k + 1) * CK] for k in range(n)]
            if diag:
                parts[-1] = jnp.where(lane <= tok, parts[-1], NEG)
            for k in range(n):
                s_s[i + k] = parts[k]
            cols = [p[:, h * D : (h + 1) * D] for p in parts for h in range(2)]
            mx[...] = functools.reduce(jnp.maximum, cols, mx[...])

        walk(scores, STEP1)
        m = jnp.max(mx[...], axis=1, keepdims=True)
        mx[...] = jnp.broadcast_to(m * C2, (ROWS, D))
        o_s[...] = jnp.zeros_like(o_s)

        def weigh(i, n, diag):
            mm = mx[...]
            mm = jnp.concatenate([mm, mm], axis=1)
            ws = [jnp.exp2(s_s[i + k] * C2 - mm).astype(BF) for k in range(n)]
            for k in range(n):
                w_s[i + k] = ws[k]
            o_s[...] += dg(jnp.concatenate(ws, axis=1), vs[chunk(i, n), :], 1, 0)

        walk(weigh, STEP2)
        inv = 1.0 / o_s[:, D:]
        att = (o_s[:, :D] * inv).astype(BF)
        gp = (ga_s[:, 0:D].astype(F32) * inv).astype(BF)
        ga_s[:, 0:D] = gp
        for h in range(HEADS):
            o_b[:, h * D : (h + 1) * D] = att[h * TB : (h + 1) * TB, :]
        delta = jnp.sum(gp.astype(F32) * att.astype(F32), axis=1, keepdims=True)
        ga_s[:, D:] = at_cols(-delta, ROWS).astype(BF)
        qt_s[...] = q_s[:, 0:D].T
        gt_s[...] = gp.T
        dq_s[...] = jnp.zeros_like(dq_s)

        def back(i, n, diag):
            dp = dg(ga_s[...], vs[chunk(i, n), :], 1, 1).astype(BF)
            ws = [w_s[i + k] for k in range(n)]
            dss = [ws[k] * dp[:, k * CK : (k + 1) * CK] for k in range(n)]
            dq_s[...] += dg(jnp.concatenate(dss, axis=1), ks[chunk(i, n), 0:D], 1, 0)
            for k in range(n):
                dkt[i + k] += dg(qt_s[...], dss[k], 1, 0)
                dvt[i + k] += dg(gt_s[...], ws[k], 1, 0)

        walk(back, STEP3)
        dqv = (dq_s[...] * SCALE).astype(BF)
        for h in range(HEADS):
            o_b[:, (HEADS + h) * D : (HEADS + h + 1) * D] = dqv[h * TB : (h + 1) * TB, :]
        for sh in range(4):

            @pl.when(lax.rem(y_me - b + 4, 4) == sh)
            def _(sh=sh):
                out_refs[sh][...] = o_b[...]

        return carry

    for fetch in fetches:
        fetch.wait()
    lax.fori_loop(0, 4, block, 0)

    for rel in range(4):
        z = zhi if rel < 2 else 1 - zhi
        c = core if rel % 2 == 0 else 1 - core
        for sh in range(4):
            yy = lax.rem(y_me - sh + 4, 4)
            i = 2 + nh1 + z * 4 + yy
            half = pl.ds(pl.multiple_of(c * 128, 128), 128)
            if last:
                ref, at = (keep_ref, send_ref)[rel % 2], rel // 2
            else:
                ref, at = (keep_ref, send_ref)[rel // 2], rel % 2
            ref[at, sh, :, 0:D] = (dkt[i, :, half] * SCALE).T.astype(BF)
            ref[at, sh, :, D:] = dvt[i, :, half].T.astype(BF)
    for i in range(4):

        @pl.when(i < 2 + nh1)
        def _(i=i):
            s_s[0, 0:CK, 0:D] = (dkt[i] * SCALE).T
            s_s[0, 0:CK, D:] = dvt[i].T
            s_s[1 + i // 2, (i % 2) * CK : (i % 2 + 1) * CK, :] = s_s[0, 0:CK, :]

    n = jnp.int32(0)
    for f in range(8):
        first = s_s[1, f * 64 : (f + 1) * 64, :]
        second = s_s[2, pl.ds(pl.multiple_of(n * 64, 64), 64), :]
        second = jnp.where(see[f], second, 0.0)
        n = n + see[f].astype(jnp.int32)
        if last:
            first = first + acc_ref[f, 0:64, :]
            second = second + acc_ref[f, 64:128, :]
            both = jnp.concatenate([first, second], axis=0).T.astype(BF)
            for p in range(4):
                hg_ref[f, p, 0] = both[p * 32 : (p + 1) * 32]
                hg_ref[f, p, 1] = both[D + p * 32 : D + (p + 1) * 32]
        else:
            hg_ref[f, 0:64, :] = first
            hg_ref[f, 64:128, :] = second


def span_call(ordinal, pos, cnt, ids, qg, gathered, acc=None):
    last = ordinal == 1
    smem = pl.BlockSpec(memory_space=pltpu.SMEM)
    vmem = pl.BlockSpec(memory_space=pltpu.VMEM)
    extra = (acc,) if last else ()
    out = (jax.ShapeDtypeStruct((TB, 2 * HEADS * D), BF),) * 4
    hg = jax.ShapeDtypeStruct((8, 4, 2, 32, TB), BF) if last else jax.ShapeDtypeStruct((8, TB, 2 * D), F32)
    return pl.pallas_call(
        functools.partial(span_kernel, ordinal),
        out_shape=out
        + (jax.ShapeDtypeStruct((2, 4, TB, 2 * D), BF),) * 2
        + (hg,),
        in_specs=[smem] * 3 + [pl.BlockSpec(memory_space=pl.ANY)] * len(qg) + [vmem] * (4 + len(extra)),
        out_specs=(vmem,) * (len(out) + 3),
        scratch_shapes=[
            pltpu.VMEM((NROW, 2 * D), BF),
            pltpu.VMEM((NROW, 2 * D), BF),
            pltpu.VMEM((ROWS, 2 * D), BF),
            pltpu.VMEM((ROWS, 2 * D), BF),
            pltpu.VMEM((D, ROWS), BF),
            pltpu.VMEM((D, ROWS), BF),
            pltpu.VMEM((NCH, ROWS, CK), F32),
            pltpu.VMEM((NCH, ROWS, CK), BF),
            pltpu.VMEM((ROWS, D), F32),
            pltpu.VMEM((ROWS, 2 * D), F32),
            pltpu.VMEM((ROWS, D), F32),
            pltpu.VMEM((NCH, D, CK), F32),
            pltpu.VMEM((NCH, D, CK), F32),
            pltpu.VMEM((4, TB, 2 * HEADS * D), BF),
            pltpu.VMEM((TB, 2 * HEADS * D), BF),
            pltpu.VMEM((4, 8, 32, 2 * D), BF),
            pltpu.SemaphoreType.DMA((4,)),
        ],
        compiler_params=pltpu.CompilerParams(vmem_limit_bytes=40 * 2**20),
        cost_estimate=pl.CostEstimate(flops=int(2.5e10), bytes_accessed=6 * 2**20, transcendentals=0),
    )(pos, cnt, ids, *qg, *gathered, *extra)


def split_shifts_kernel(pos_ref, a_ref, b_ref, *outs):
    for sh in range(4):
        at = pl.ds(pl.multiple_of(lax.rem(pos_ref[1] + sh, 4) * D, D), D)
        for j in range(2):
            outs[sh][j, :, 0:D] = a_ref[0, j, :, at]
            outs[sh][j, :, D:] = b_ref[0, j, :, at]


def join_shifts_kernel(pos_ref, p0, p1, p2, p3, a_ref, b_ref):
    for sh, part in enumerate((p0, p1, p2, p3)):
        at = pl.ds(pl.multiple_of(lax.rem(pos_ref[1] + sh, 4) * D, D), D)
        for j in range(2):
            a_ref[0, j, :, at] = part[j, :, 0:D]
            b_ref[0, j, :, at] = part[j, :, D:]


def copy_all(pairs, sem):
    copies = [pltpu.make_async_copy(src, dst, sem.at[i]) for i, (src, dst) in enumerate(pairs)]
    for c in copies:
        c.start()
    for c in copies:
        c.wait()


def split_heads_kernel(pos_ref, a_ref, b_ref, out0, s0, s1, s2, s3, sem):
    width = HEADS * D
    pairs = []
    for y in range(4):
        at = pl.ds(y * width, width)
        pairs.append((a_ref.at[0, 0, :, at], out0.at[y, :, pl.ds(0, width)]))
        pairs.append((b_ref.at[0, 0, :, at], out0.at[y, :, pl.ds(width, width)]))
    for sh, part in enumerate((s0, s1, s2, s3)):
        at = pl.ds(pl.multiple_of(lax.rem(pos_ref[1] + sh, 4) * width, D), width)
        pairs.append((a_ref.at[0, 1, :, at], part.at[:, pl.ds(0, width)]))
        pairs.append((b_ref.at[0, 1, :, at], part.at[:, pl.ds(width, width)]))
    copy_all(pairs, sem)


def join_heads_kernel(pos_ref, *refs):
    width = HEADS * D
    a_ref, b_ref, sem = refs[8:]
    pairs = []
    for sh in range(4):
        at = pl.ds(pl.multiple_of(lax.rem(pos_ref[1] + sh, 4) * width, D), width)
        for j in range(2):
            pairs.append((refs[4 * j + sh].at[:, pl.ds(0, width)], a_ref.at[0, j, :, at]))
            pairs.append((refs[4 * j + sh].at[:, pl.ds(width, width)], b_ref.at[0, j, :, at]))
    copy_all(pairs, sem)


def relayout(kernel, outs, args, with_pos, copies=0):
    ref = pl.BlockSpec(memory_space=pl.ANY if copies else pltpu.VMEM)
    specs = [ref] * len(args)
    if with_pos:
        specs[0] = pl.BlockSpec(memory_space=pltpu.SMEM)
    size = 2 * sum(a.size * 2 for a in args)
    return pl.pallas_call(
        kernel,
        out_shape=tuple(jax.ShapeDtypeStruct(o, BF) for o in outs),
        in_specs=specs,
        out_specs=(ref,) * len(outs),
        scratch_shapes=[pltpu.SemaphoreType.DMA((copies,))] if copies else [],
        cost_estimate=pl.CostEstimate(flops=0, bytes_accessed=size, transcendentals=0),
        compiler_params=pltpu.CompilerParams(vmem_limit_bytes=16 * 2**20),
    )(*args)


def y_exchange(a):
    return lax.all_to_all(a, "y", split_axis=0, concat_axis=0, tiled=True)


def y_shift(a, sh):
    return lax.ppermute(a, "y", [(i, (i + sh) % 4) for i in range(4)])


def flip(a, axis):
    return lax.ppermute(a, axis, [(0, 1), (1, 0)])


def linear(z, y, c):
    return z * 8 + y * 2 + c


def per_device(queries, span_keys, span_values, cotangent, cache_keys, cache_values, hist_count, span_ids):
    zhi, y_me, core = lax.axis_index("zhi"), lax.axis_index("y"), lax.axis_index("core")
    pos = jnp.stack([zhi, y_me, core, lax.axis_index("x"), lax.axis_index("zlo")]).astype(jnp.int32)

    cache = jnp.concatenate([cache_keys.T, cache_values.T], axis=1)
    perm = []
    for head in range(KVH):
        for p in range(4):
            perm.append((linear(head // 2, 2 * (head % 2) + p // 2, p % 2), linear(p // 2, head, p % 2)))
    cache = lax.ppermute(cache, SP, perm)
    cache = jnp.stack([cache] + [lax.ppermute(cache, "x", [(i, (i + s) % 4) for i in range(4)]) for s in (1, 2, 3)])
    cache_x = cache
    cache = jnp.stack([cache, flip(cache, "zlo")]).reshape(8 * 32, 2 * D)
    kv_sent = relayout(split_shifts_kernel, [(2, TB, 2 * D)] * 4, (pos, span_keys, span_values), True)
    queries, kv_sent = lax.optimization_barrier((queries, kv_sent))
    wide = (TB, 2 * HEADS * D)
    sent0, *sent1 = relayout(
        split_heads_kernel, [(4,) + wide] + [wide] * 4, (pos, queries, cotangent), True, 16
    )
    kv_here = [kv_sent[0]] + [y_shift(kv_sent[sh], sh) for sh in (1, 2, 3)]
    own = jnp.concatenate([a[0] for a in kv_here] + [cache] + [a[1] for a in kv_here], axis=0)
    sent0, own = lax.optimization_barrier((sent0, own))
    qg0 = y_exchange(sent0)
    other = flip(own, "zhi")
    gathered = (own, flip(own, "core"), other, flip(other, "core"))
    sent1, _ = lax.optimization_barrier((sent1, other))
    qg1 = [sent1[0]] + [y_shift(sent1[sh], sh) for sh in (1, 2, 3)]
    out0 = span_call(0, pos, hist_count, span_ids, (qg0,), gathered)
    *out0, keep0, send0, acc = out0
    *out1, keep1, send1, hg = span_call(1, pos, hist_count, span_ids, qg1, gathered, acc)

    back0 = [out0[0]] + [y_shift(out0[sh], 4 - sh) for sh in (1, 2, 3)]
    got0 = flip(send0, "zhi")
    (out1, send1, hg, back0, got0) = lax.optimization_barrier((out1, send1, hg, back0, got0))
    sum0 = (keep0.astype(F32) + got0.astype(F32)).astype(BF)
    got1 = flip(send1, "core")
    back1 = [out1[0]] + [y_shift(out1[sh], 4 - sh) for sh in (1, 2, 3)]
    sum1 = (keep1.astype(F32) + got1.astype(F32)).astype(BF)
    hg, sum1 = lax.optimization_barrier((hg, sum1))
    hg = lax.all_to_all(hg.reshape(32, 2, 32, TB), FS + ("zhi", "core"), split_axis=0, concat_axis=0, tiled=True)
    got0 = flip(sum0[1], "core")
    got1 = flip(sum1[1], "zhi")
    red0 = sum0[0].astype(F32) + got0.astype(F32)
    red1 = sum1[0].astype(F32) + got1.astype(F32)
    red = jnp.stack([red0, red1], axis=1).astype(BF)
    back1, red = lax.optimization_barrier((back1, red))
    kv_back = [red[0]] + [y_shift(red[sh], 4 - sh) for sh in (1, 2, 3)]

    hgrad = lax.ppermute(jnp.sum(hg.astype(F32), axis=0), SP, [(b, a) for a, b in perm])
    attended, grad_q = relayout(join_heads_kernel, [(1, 2, TB, 4 * HEADS * D)] * 2, (pos, *back0, *back1), True, 16)
    grad_k, grad_v = relayout(join_shifts_kernel, [(1, 2, TB, 4 * D)] * 2, (pos, *kv_back), True)
    return attended, grad_q, grad_k, grad_v, hgrad[0].T, hgrad[1].T


def solution(mesh):
    fine = Mesh(mesh.devices.reshape(4, 2, 2, 4, 2), ("x", "zlo", "zhi", "y", "core"))
    tokens = P(FS, None, SP, None)
    resident = P(FS, SP)
    return jax.shard_map(
        per_device,
        mesh=fine,
        in_specs=(tokens,) * 4 + (resident,) * 2 + (P(), P()),
        out_specs=(tokens,) * 4 + (resident,) * 2,
        check_vma=False,
    )
```

```python
import functools
import math

import jax
import jax.numpy as jnp
from jax import lax
from jax.experimental import pallas as pl
from jax.experimental.pallas import tpu as pltpu
from jax.sharding import Mesh
from jax.sharding import PartitionSpec as P

BF = jnp.bfloat16
F32 = jnp.float32
HEADS = 4
KVH = 4
D = 128
TB = 128
ROWS = HEADS * TB
CK = 256
HIST = 1024
SPAN = 2048
NROW = HIST + SPAN
NCH = NROW // CK
SCALE = 1.0 / math.sqrt(D)
C2 = SCALE * math.log2(math.e)
NEG = -1e30
STEP1, STEP2, STEP3 = 5, 5, 5
SP = ("zhi", "y", "core")
FS = ("x", "zlo")


def dg(a, b, ca, cb):
    return lax.dot_general(a, b, (((ca,), (cb,)), ((), ())), preferred_element_type=F32)


def pieces(x):
    a = x.astype(BF)
    r = x - a.astype(F32)
    b = r.astype(BF)
    c = (r - b.astype(F32)).astype(BF)
    return a, b, c


def at_cols(x, rows):
    ln = lax.broadcasted_iota(jnp.int32, (rows, D), 1)
    out = jnp.zeros((rows, D), F32)
    for k, p in enumerate(pieces(x)):
        out = jnp.where(ln == k, p.astype(F32), out)
    return out


def span_kernel(
    ordinal, pos_ref, cnt_ref, ids_ref, *rest
):
    last = ordinal == 1
    qg_hbm, rest = (rest[:4], rest[4:]) if last else (rest[:1], rest[1:])
    gathered, rest = rest[:4], rest[4:]
    if last:
        acc_ref, *rest = rest
    first_kv = ordinal * (4 * TB + 8 * 32)
    *out_refs, keep_ref, send_ref, hg_ref = rest[:7]
    rest = rest[7:]
    (ks, vs, q_s, ga_s, qt_s, gt_s, s_s, w_s, mx, o_s, dq_s, dkt, dvt, qg_ref, o_b, h_s, sem) = rest
    zhi, y_me, core, x_me, zlo = pos_ref[0], pos_ref[1], pos_ref[2], pos_ref[3], pos_ref[4]
    f_me = x_me * 2 + zlo
    if last:
        fetches = [
            pltpu.make_async_copy(qg_hbm[sh], qg_ref.at[lax.rem(y_me - sh + 4, 4)], sem.at[sh]) for sh in range(4)
        ]
    else:
        fetches = [pltpu.make_async_copy(qg_hbm[0], qg_ref, sem.at[0])]
    for fetch in fetches:
        fetch.start()
    span_id = ids_ref[f_me, ordinal]
    see = [(cnt_ref[f] > 1) & (f + 8 < span_id) for f in range(8)]
    vs[:, D:] = jnp.ones((NROW, D), BF)
    n1 = jnp.int32(0)
    for f in range(8):
        n1 = n1 + see[f].astype(jnp.int32)
    nh1 = (n1 + 3) // 4
    ln = lax.broadcasted_iota(jnp.int32, (HIST, D), 1)
    rw = lax.broadcasted_iota(jnp.int32, (HIST, D), 0)
    ks[0:HIST, D:] = jnp.where((ln == 0) & (rw >= 512 + n1 * 64), NEG, 0.0).astype(BF)
    base = pl.multiple_of(512 + nh1 * CK, CK)
    n = jnp.int32(0)

    for rel in range(4):
        for i in range(8):
            h_s[rel, i] = gathered[rel][4 * TB + i * 32 : 4 * TB + (i + 1) * 32, :]

    def history(f, piece):
        rel = (zhi ^ (piece // 2)) * 2 + (core ^ (piece % 2))
        return h_s[rel, (zlo ^ (f % 2)) * 4 + lax.rem(x_me - f // 2 + 4, 4)]

    for f in range(8):
        cols = jnp.concatenate([history(f, p) for p in range(4)], axis=0)
        rows = jnp.concatenate([cols[:, 0:TB].T, cols[:, TB:].T], axis=1)
        ks[f * 64 : (f + 1) * 64, 0:D] = rows[0:64, 0:D]
        vs[f * 64 : (f + 1) * 64, 0:D] = rows[0:64, D:]
        at = pl.multiple_of(512 + n * 64, 64)
        ks[pl.ds(at, 64), 0:D] = rows[64:, 0:D]
        vs[pl.ds(at, 64), 0:D] = rows[64:, D:]
        n = n + see[f].astype(jnp.int32)
    for r in range(4):

        @pl.when(n1 + r < nh1 * 4)
        def _(r=r):
            at = pl.multiple_of(512 + (n1 + r) * 64, 64)
            ks[pl.ds(at, 64), 0:D] = jnp.zeros((64, D), BF)
            vs[pl.ds(at, 64), 0:D] = jnp.zeros((64, D), BF)

    for rel in range(4):
        z = zhi if rel < 2 else 1 - zhi
        c = core if rel % 2 == 0 else 1 - core
        for sh in range(4):
            yy = lax.rem(y_me - sh + 4, 4)
            at = pl.multiple_of(base + z * 1024 + yy * 256 + c * 128, 128)
            part = gathered[rel][first_kv + sh * TB : first_kv + (sh + 1) * TB, :]
            ks[pl.ds(at, 128), 0:D] = part[:, 0:D]
            ks[pl.ds(at, 128), D:] = jnp.zeros((128, D), BF)
            vs[pl.ds(at, 128), 0:D] = part[:, D:]
    dkt[...] = jnp.zeros_like(dkt)
    dvt[...] = jnp.zeros_like(dvt)
    lnr = lax.broadcasted_iota(jnp.int32, (ROWS, D), 1)
    lane = lax.broadcasted_iota(jnp.int32, (ROWS, CK), 1)
    tok = lax.broadcasted_iota(jnp.int32, (ROWS, CK), 0) % TB + core * TB
    q_s[:, D:] = jnp.where(lnr == 0, 1.0, 0.0).astype(BF)

    def chunk(i, n):
        return pl.ds(pl.multiple_of(i * CK, CK), n * CK)

    def block(b, carry):
        for h in range(HEADS):
            q_s[h * TB : (h + 1) * TB, 0:D] = qg_ref[b, :, h * D : (h + 1) * D]
            ga_s[h * TB : (h + 1) * TB, 0:D] = qg_ref[b, :, (HEADS + h) * D : (HEADS + h + 1) * D]
        mx[...] = jnp.full_like(mx, NEG)
        nfull = 2 + nh1 + zhi * 4 + b

        def walk(fn, step):
            groups = nfull // step

            def one(i, carry):
                fn(step * i, step, False)
                return carry

            lax.fori_loop(0, groups, one, 0)
            for r in range(step):

                @pl.when(nfull - groups * step == r)
                def _(r=r):
                    fn(nfull - r, r + 1, True)

        def scores(i, n, diag):
            s = dg(q_s[...], ks[chunk(i, n), :], 1, 1)
            parts = [s[:, k * CK : (k + 1) * CK] for k in range(n)]
            if diag:
                parts[-1] = jnp.where(lane <= tok, parts[-1], NEG)
            for k in range(n):
                s_s[i + k] = parts[k]
            cols = [p[:, h * D : (h + 1) * D] for p in parts for h in range(2)]
            mx[...] = functools.reduce(jnp.maximum, cols, mx[...])

        walk(scores, STEP1)
        m = jnp.max(mx[...], axis=1, keepdims=True)
        mx[...] = jnp.broadcast_to(m * C2, (ROWS, D))
        o_s[...] = jnp.zeros_like(o_s)

        def weigh(i, n, diag):
            mm = mx[...]
            mm = jnp.concatenate([mm, mm], axis=1)
            ws = [jnp.exp2(s_s[i + k] * C2 - mm).astype(BF) for k in range(n)]
            for k in range(n):
                w_s[i + k] = ws[k]
            o_s[...] += dg(jnp.concatenate(ws, axis=1), vs[chunk(i, n), :], 1, 0)

        walk(weigh, STEP2)
        inv = 1.0 / o_s[:, D:]
        att = (o_s[:, :D] * inv).astype(BF)
        gp = (ga_s[:, 0:D].astype(F32) * inv).astype(BF)
        ga_s[:, 0:D] = gp
        for h in range(HEADS):
            o_b[:, h * D : (h + 1) * D] = att[h * TB : (h + 1) * TB, :]
        delta = jnp.sum(gp.astype(F32) * att.astype(F32), axis=1, keepdims=True)
        ga_s[:, D:] = at_cols(-delta, ROWS).astype(BF)
        qt_s[...] = q_s[:, 0:D].T
        gt_s[...] = gp.T
        dq_s[...] = jnp.zeros_like(dq_s)

        def back(i, n, diag):
            dp = dg(ga_s[...], vs[chunk(i, n), :], 1, 1).astype(BF)
            ws = [w_s[i + k] for k in range(n)]
            dss = [ws[k] * dp[:, k * CK : (k + 1) * CK] for k in range(n)]
            dq_s[...] += dg(jnp.concatenate(dss, axis=1), ks[chunk(i, n), 0:D], 1, 0)
            for k in range(n):
                dkt[i + k] += dg(qt_s[...], dss[k], 1, 0)
                dvt[i + k] += dg(gt_s[...], ws[k], 1, 0)

        walk(back, STEP3)
        dqv = (dq_s[...] * SCALE).astype(BF)
        for h in range(HEADS):
            o_b[:, (HEADS + h) * D : (HEADS + h + 1) * D] = dqv[h * TB : (h + 1) * TB, :]
        for sh in range(4):

            @pl.when(lax.rem(y_me - b + 4, 4) == sh)
            def _(sh=sh):
                out_refs[sh][...] = o_b[...]

        return carry

    for fetch in fetches:
        fetch.wait()
    lax.fori_loop(0, 4, block, 0)

    for rel in range(4):
        z = zhi if rel < 2 else 1 - zhi
        c = core if rel % 2 == 0 else 1 - core
        for sh in range(4):
            yy = lax.rem(y_me - sh + 4, 4)
            i = 2 + nh1 + z * 4 + yy
            half = pl.ds(pl.multiple_of(c * 128, 128), 128)
            if last:
                ref, at = (keep_ref, send_ref)[rel % 2], rel // 2
            else:
                ref, at = (keep_ref, send_ref)[rel // 2], rel % 2
            ref[at, sh, :, 0:D] = (dkt[i, :, half] * SCALE).T.astype(BF)
            ref[at, sh, :, D:] = dvt[i, :, half].T.astype(BF)
    for i in range(4):

        @pl.when(i < 2 + nh1)
        def _(i=i):
            s_s[0, 0:CK, 0:D] = (dkt[i] * SCALE).T
            s_s[0, 0:CK, D:] = dvt[i].T
            s_s[1 + i // 2, (i % 2) * CK : (i % 2 + 1) * CK, :] = s_s[0, 0:CK, :]

    n = jnp.int32(0)
    for f in range(8):
        first = s_s[1, f * 64 : (f + 1) * 64, :]
        second = s_s[2, pl.ds(pl.multiple_of(n * 64, 64), 64), :]
        second = jnp.where(see[f], second, 0.0)
        n = n + see[f].astype(jnp.int32)
        if last:
            first = first + acc_ref[f, 0:64, :]
            second = second + acc_ref[f, 64:128, :]
            both = jnp.concatenate([first, second], axis=0).T.astype(BF)
            for p in range(4):
                hg_ref[f, p, 0] = both[p * 32 : (p + 1) * 32]
                hg_ref[f, p, 1] = both[D + p * 32 : D + (p + 1) * 32]
        else:
            hg_ref[f, 0:64, :] = first
            hg_ref[f, 64:128, :] = second


def span_call(ordinal, pos, cnt, ids, qg, gathered, acc=None):
    last = ordinal == 1
    smem = pl.BlockSpec(memory_space=pltpu.SMEM)
    vmem = pl.BlockSpec(memory_space=pltpu.VMEM)
    extra = (acc,) if last else ()
    out = (jax.ShapeDtypeStruct((TB, 2 * HEADS * D), BF),) * 4
    hg = jax.ShapeDtypeStruct((8, 4, 2, 32, TB), BF) if last else jax.ShapeDtypeStruct((8, TB, 2 * D), F32)
    return pl.pallas_call(
        functools.partial(span_kernel, ordinal),
        out_shape=out
        + (jax.ShapeDtypeStruct((2, 4, TB, 2 * D), BF),) * 2
        + (hg,),
        in_specs=[smem] * 3 + [pl.BlockSpec(memory_space=pl.ANY)] * len(qg) + [vmem] * (4 + len(extra)),
        out_specs=(vmem,) * (len(out) + 3),
        scratch_shapes=[
            pltpu.VMEM((NROW, 2 * D), BF),
            pltpu.VMEM((NROW, 2 * D), BF),
            pltpu.VMEM((ROWS, 2 * D), BF),
            pltpu.VMEM((ROWS, 2 * D), BF),
            pltpu.VMEM((D, ROWS), BF),
            pltpu.VMEM((D, ROWS), BF),
            pltpu.VMEM((NCH, ROWS, CK), F32),
            pltpu.VMEM((NCH, ROWS, CK), BF),
            pltpu.VMEM((ROWS, D), F32),
            pltpu.VMEM((ROWS, 2 * D), F32),
            pltpu.VMEM((ROWS, D), F32),
            pltpu.VMEM((NCH, D, CK), F32),
            pltpu.VMEM((NCH, D, CK), F32),
            pltpu.VMEM((4, TB, 2 * HEADS * D), BF),
            pltpu.VMEM((TB, 2 * HEADS * D), BF),
            pltpu.VMEM((4, 8, 32, 2 * D), BF),
            pltpu.SemaphoreType.DMA((4,)),
        ],
        compiler_params=pltpu.CompilerParams(vmem_limit_bytes=40 * 2**20),
        cost_estimate=pl.CostEstimate(flops=int(2.5e10), bytes_accessed=6 * 2**20, transcendentals=0),
    )(pos, cnt, ids, *qg, *gathered, *extra)


def split_shifts_kernel(pos_ref, a_ref, b_ref, *outs):
    for sh in range(4):
        at = pl.ds(pl.multiple_of(lax.rem(pos_ref[1] + sh, 4) * D, D), D)
        for j in range(2):
            outs[sh][j, :, 0:D] = a_ref[0, j, :, at]
            outs[sh][j, :, D:] = b_ref[0, j, :, at]


def join_shifts_kernel(pos_ref, p0, p1, p2, p3, a_ref, b_ref):
    for sh, part in enumerate((p0, p1, p2, p3)):
        at = pl.ds(pl.multiple_of(lax.rem(pos_ref[1] + sh, 4) * D, D), D)
        for j in range(2):
            a_ref[0, j, :, at] = part[j, :, 0:D]
            b_ref[0, j, :, at] = part[j, :, D:]


def copy_all(pairs, sem):
    copies = [pltpu.make_async_copy(src, dst, sem.at[i]) for i, (src, dst) in enumerate(pairs)]
    for c in copies:
        c.start()
    for c in copies:
        c.wait()


def split_heads_kernel(pos_ref, a_ref, b_ref, out0, s0, s1, s2, s3, sem):
    width = HEADS * D
    pairs = []
    for y in range(4):
        at = pl.ds(y * width, width)
        pairs.append((a_ref.at[0, 0, :, at], out0.at[y, :, pl.ds(0, width)]))
        pairs.append((b_ref.at[0, 0, :, at], out0.at[y, :, pl.ds(width, width)]))
    for sh, part in enumerate((s0, s1, s2, s3)):
        at = pl.ds(pl.multiple_of(lax.rem(pos_ref[1] + sh, 4) * width, D), width)
        pairs.append((a_ref.at[0, 1, :, at], part.at[:, pl.ds(0, width)]))
        pairs.append((b_ref.at[0, 1, :, at], part.at[:, pl.ds(width, width)]))
    copy_all(pairs, sem)


def join_heads_kernel(pos_ref, *refs):
    width = HEADS * D
    a_ref, b_ref, sem = refs[8:]
    pairs = []
    for sh in range(4):
        at = pl.ds(pl.multiple_of(lax.rem(pos_ref[1] + sh, 4) * width, D), width)
        for j in range(2):
            pairs.append((refs[4 * j + sh].at[:, pl.ds(0, width)], a_ref.at[0, j, :, at]))
            pairs.append((refs[4 * j + sh].at[:, pl.ds(width, width)], b_ref.at[0, j, :, at]))
    copy_all(pairs, sem)


def relayout(kernel, outs, args, with_pos, copies=0):
    ref = pl.BlockSpec(memory_space=pl.ANY if copies else pltpu.VMEM)
    specs = [ref] * len(args)
    if with_pos:
        specs[0] = pl.BlockSpec(memory_space=pltpu.SMEM)
    size = 2 * sum(a.size * 2 for a in args)
    return pl.pallas_call(
        kernel,
        out_shape=tuple(jax.ShapeDtypeStruct(o, BF) for o in outs),
        in_specs=specs,
        out_specs=(ref,) * len(outs),
        scratch_shapes=[pltpu.SemaphoreType.DMA((copies,))] if copies else [],
        cost_estimate=pl.CostEstimate(flops=0, bytes_accessed=size, transcendentals=0),
        compiler_params=pltpu.CompilerParams(vmem_limit_bytes=16 * 2**20),
    )(*args)


def y_exchange(a):
    return lax.all_to_all(a, "y", split_axis=0, concat_axis=0, tiled=True)


def y_shift(a, sh):
    return lax.ppermute(a, "y", [(i, (i + sh) % 4) for i in range(4)])


def flip(a, axis):
    return lax.ppermute(a, axis, [(0, 1), (1, 0)])


def linear(z, y, c):
    return z * 8 + y * 2 + c


def per_device(queries, span_keys, span_values, cotangent, cache_keys, cache_values, hist_count, span_ids):
    zhi, y_me, core = lax.axis_index("zhi"), lax.axis_index("y"), lax.axis_index("core")
    pos = jnp.stack([zhi, y_me, core, lax.axis_index("x"), lax.axis_index("zlo")]).astype(jnp.int32)

    cache = jnp.concatenate([cache_keys.T, cache_values.T], axis=1)
    perm = []
    for head in range(KVH):
        for p in range(4):
            perm.append((linear(head // 2, 2 * (head % 2) + p // 2, p % 2), linear(p // 2, head, p % 2)))
    cache = lax.ppermute(cache, SP, perm)
    cache = jnp.stack([cache] + [lax.ppermute(cache, "x", [(i, (i + s) % 4) for i in range(4)]) for s in (1, 2, 3)])
    cache_x = cache
    cache = jnp.stack([cache, flip(cache, "zlo")]).reshape(8 * 32, 2 * D)
    kv_sent = relayout(split_shifts_kernel, [(2, TB, 2 * D)] * 4, (pos, span_keys, span_values), True)
    queries, kv_sent = lax.optimization_barrier((queries, kv_sent))
    wide = (TB, 2 * HEADS * D)
    sent0, *sent1 = relayout(
        split_heads_kernel, [(4,) + wide] + [wide] * 4, (pos, queries, cotangent), True, 16
    )
    kv_here = [kv_sent[0]] + [y_shift(kv_sent[sh], sh) for sh in (1, 2, 3)]
    own = jnp.concatenate([a[0] for a in kv_here] + [cache] + [a[1] for a in kv_here], axis=0)
    sent0, own = lax.optimization_barrier((sent0, own))
    qg0 = y_exchange(sent0)
    other = flip(own, "zhi")
    gathered = (own, flip(own, "core"), other, flip(other, "core"))
    sent1, _ = lax.optimization_barrier((sent1, other))
    qg1 = [sent1[0]] + [y_shift(sent1[sh], sh) for sh in (1, 2, 3)]
    out0 = span_call(0, pos, hist_count, span_ids, (qg0,), gathered)
    *out0, keep0, send0, acc = out0
    *out1, keep1, send1, hg = span_call(1, pos, hist_count, span_ids, qg1, gathered, acc)

    back0 = [out0[0]] + [y_shift(out0[sh], 4 - sh) for sh in (1, 2, 3)]
    got0 = flip(send0, "zhi")
    (out1, send1, hg, back0, got0) = lax.optimization_barrier((out1, send1, hg, back0, got0))
    here0 = keep0[0].astype(F32) + got0[0].astype(F32)
    away0 = (keep0[1].astype(F32) + got0[1].astype(F32)).astype(BF)
    got1 = flip(send1, "core")
    back1 = [out1[0]] + [y_shift(out1[sh], 4 - sh) for sh in (1, 2, 3)]
    here1 = keep1[0].astype(F32) + got1[0].astype(F32)
    away1 = (keep1[1].astype(F32) + got1[1].astype(F32)).astype(BF)
    hg, away1 = lax.optimization_barrier((hg, away1))
    hg = lax.all_to_all(hg.reshape(32, 2, 32, TB), FS + ("zhi", "core"), split_axis=0, concat_axis=0, tiled=True)
    got0 = flip(away0, "core")
    got1 = flip(away1, "zhi")
    red0 = here0 + got0.astype(F32)
    red1 = here1 + got1.astype(F32)
    red = jnp.stack([red0, red1], axis=1).astype(BF)
    back1, red = lax.optimization_barrier((back1, red))
    kv_back = [red[0]] + [y_shift(red[sh], 4 - sh) for sh in (1, 2, 3)]

    hgrad = lax.ppermute(jnp.sum(hg.astype(F32), axis=0), SP, [(b, a) for a, b in perm])
    attended, grad_q = relayout(join_heads_kernel, [(1, 2, TB, 4 * HEADS * D)] * 2, (pos, *back0, *back1), True, 16)
    grad_k, grad_v = relayout(join_shifts_kernel, [(1, 2, TB, 4 * D)] * 2, (pos, *kv_back), True)
    return attended, grad_q, grad_k, grad_v, hgrad[0].T, hgrad[1].T


def solution(mesh):
    fine = Mesh(mesh.devices.reshape(4, 2, 2, 4, 2), ("x", "zlo", "zhi", "y", "core"))
    tokens = P(FS, None, SP, None)
    resident = P(FS, SP)
    return jax.shard_map(
        per_device,
        mesh=fine,
        in_specs=(tokens,) * 4 + (resident,) * 2 + (P(), P()),
        out_specs=(tokens,) * 4 + (resident,) * 2,
        check_vma=False,
    )
```
